32 devices in a mesh: row: 8 (over z, x), col: 4 (over y, core).
Axes of the slice: x: 2, y: 2, z: 4, core: 2. Of those that a mesh axis runs over, the one named last changes fastest.
Arguments:
- log_rate: float32 [131072], P(('row', 'col')), may hold values from -0.5 to 1
- state: float32 [131072], P(('row', 'col')), may hold values from 0.2 to 1
- excess: float32 [131072], P(('row', 'col')), may hold values from -0.3 to 0.3
- normal_stress: float32 [131072], P(('row', 'col')), may hold values from 2 to 4
- rate_param: float32 [131072], P(('row', 'col')), may hold values from 0.5 to 1
- state_param: float32 [131072], P(('row', 'col')), may hold values from 0.5 to 1.5
- slip_length: float32 [131072], P(('row', 'col')), may hold values from 1 to 4
- self_stiffness: float32 [131072], P(('row', 'col')), may hold values from 0.2 to 1
- damping: float32 [131072], P(('row', 'col')), may hold values from 1 to 2
- blocks: bfloat16 [8, 4, 512, 4096], P('row', 'col'), may hold values from -0.1796875 to 0.1796875
- pattern: int32 [8, 4, 512, 2], P('row', 'col'), may hold values from 0 to 511, as said below
- counts: int32 [8, 4], P('row', 'col'), may hold values from 1 to 512, as said below
Outputs:
- final_log_rate: float32 [131072], P(('row', 'col'))
- final_state: float32 [131072], P(('row', 'col'))
- final_stress: float32 [131072], P(('row', 'col'))
The draws below stay inside these ranges and needn't reach their ends.
Inputs may be any that keep to these rules, and one draw needn't show every extreme that they name: Each slot (i, j) has global block row I no larger than global block column J (upper pattern, I and J as in the reference program); the same position may be stored in several slots, whose tiles then add; slots at or past the device's count hold valid indices that are ignored. `counts`: every device holds at least one live tile; some device of the first index of row holds 512.
All inputs are finite; a program needn't handle non-finite values.
Results may differ from the reference program's by a relative error of at most 0.0014.
Values may be sent and summed in bfloat16 or wider, within the bound.
A program may use at most 64 MiB of HBM per device.

```python
import math
import jax
import jax.numpy as jnp
from jax import lax

PATCH_DEV = 4096
NB_DEV = 512
STEPS = 2
NEWTON = 4
PATCHES = 131072
N_ROW = 8
N_COL = 4


def block_layout(key):
    key = jax.random.fold_in(key, 4242)
    keys = jax.random.split(key, 5)
    per_seg = PATCH_DEV // 64
    shape = (N_ROW, N_COL, NB_DEV)
    row_ids = jnp.arange(N_ROW, dtype=jnp.int32)
    col_ids = jnp.arange(N_COL, dtype=jnp.int32)
    top_load = jnp.maximum(1, NB_DEV * (N_ROW - row_ids) // N_ROW)
    top_load = jnp.broadcast_to(top_load[:, None], (N_ROW, N_COL))
    low_load = jnp.maximum(1, top_load // 2)
    loads = jax.random.randint(keys[0], (N_ROW, N_COL), low_load, top_load + 1)
    busiest = jax.random.randint(keys[1], (), 0, N_COL)
    heavy = (row_ids[:, None] == 0) & (col_ids[None, :] == busiest)
    loads = jnp.where(heavy, NB_DEV, loads)
    rows_b = jnp.broadcast_to(row_ids[:, None, None], shape)
    cols_b = jnp.broadcast_to(col_ids[None, :, None], shape)
    far_row = jax.random.randint(keys[2], shape, rows_b, N_ROW)
    offset = jax.random.randint(keys[3], shape, 0, per_seg)
    raw_row = jax.random.randint(keys[4], shape, 0, N_COL * per_seg)
    limit_row = cols_b * per_seg + offset
    bad = (far_row == rows_b) & (raw_row > limit_row)
    row_slot = jnp.where(bad, raw_row % (limit_row + 1), raw_row)
    col_slot = far_row * per_seg + offset
    pattern = jnp.stack([row_slot, col_slot], axis=-1).astype(jnp.int32)
    return (pattern, loads.astype(jnp.int32))


def draw_pattern(key, part):
    return block_layout(key)[0]


def draw_counts(key, part):
    return block_layout(key)[1]


def block_levels(key, extent, cuts, smallest, top_value):
    level = 1.0
    for dim, shards_of in cuts:
        heights = jax.random.uniform(jax.random.fold_in(jax.random.fold_in(key, 6), dim), (shards_of,), jnp.float32, smallest / len(cuts), top_value / len(cuts))
        level = level * jnp.repeat(jnp.exp(heights), extent[dim] // shards_of).reshape((-1,) + (1,) * (len(extent) - 1 - dim))
    return level


def centred(stream_key, extent, width, reach, cuts=(), held_as=jnp.bfloat16):
    gain = block_levels(stream_key, extent, cuts, -0.22, 0.18) if cuts else 1.0
    result = jax.random.normal(stream_key, extent, jnp.float32) * width * gain
    return jnp.minimum(jnp.maximum(result, -reach), reach).astype(held_as)


def setup_inputs(seed: int = 0) -> dict:
    streams_of = jax.random.split(jax.random.key(seed), 13)
    return {
        "log_rate": jnp.clip(-0.5 + 1.5 * jax.random.uniform(streams_of[0], (PATCHES,), jnp.float32) ** block_levels(streams_of[0], (PATCHES,), ((0, 32),), -0.2, 0.2), -0.5, 1.0),
        "state": jnp.clip(0.2 + 0.8 * jax.random.uniform(streams_of[1], (PATCHES,), jnp.float32) ** block_levels(streams_of[1], (PATCHES,), ((0, 32),), -0.2, 0.2), 0.2, 1.0),
        "excess": jnp.clip(jax.random.uniform(streams_of[2], (PATCHES,), jnp.float32, -0.3, 0.3) * block_levels(streams_of[2], (PATCHES,), ((0, 32),), -0.4, 0.0), -0.3, 0.3),
        "normal_stress": jnp.clip(jnp.exp(math.log(4.0) - 0.6931472 * jax.random.uniform(streams_of[3], (PATCHES,), jnp.float32) ** block_levels(streams_of[3], (PATCHES,), ((0, 32),), -0.2, 0.2)), 2.0, 4.0),
        "rate_param": jnp.clip(jnp.exp(math.log(1.0) - 0.6931472 * jax.random.uniform(streams_of[4], (PATCHES,), jnp.float32) ** block_levels(streams_of[4], (PATCHES,), ((0, 32),), -0.2, 0.2)), 0.5, 1.0),
        "state_param": jnp.clip(jnp.exp(math.log(1.5) - 1.0986123 * jax.random.uniform(streams_of[5], (PATCHES,), jnp.float32) ** block_levels(streams_of[5], (PATCHES,), ((0, 32),), -0.2, 0.2)), 0.5, 1.5),
        "slip_length": jnp.clip(jnp.exp(math.log(4.0) - 1.3862944 * jax.random.uniform(streams_of[6], (PATCHES,), jnp.float32) ** block_levels(streams_of[6], (PATCHES,), ((0, 32),), -0.2, 0.2)), 1.0, 4.0),
        "self_stiffness": jnp.clip(jnp.exp(math.log(1.0) - 1.609438 * jax.random.uniform(streams_of[7], (PATCHES,), jnp.float32) ** block_levels(streams_of[7], (PATCHES,), ((0, 32),), -0.2, 0.2)), 0.2, 1.0),
        "damping": jnp.clip(jnp.exp(math.log(2.0) - 0.6931472 * jax.random.uniform(streams_of[8], (PATCHES,), jnp.float32) ** block_levels(streams_of[8], (PATCHES,), ((0, 32),), -0.2, 0.2)), 1.0, 2.0),
        "blocks": centred(streams_of[9], (N_ROW, N_COL, NB_DEV, 4096), 0.03, 0.1796875, ((0, 8), (1, 4))),
        "pattern": draw_pattern(jax.random.fold_in(streams_of[12], 71), 0),
        "counts": draw_counts(jax.random.fold_in(streams_of[12], 71), 0),
    }


time_step = 0.25

def inverse_sinh(value):
    return jnp.log(value + jnp.sqrt(1.0 + value * value))

def apply_kernel(pushed, blocks, pattern, counts):
    per_seg = PATCH_DEV // 64
    pieces = pushed.astype(jnp.float32).reshape(-1, 64)
    tiles_all = blocks.reshape(N_ROW * N_COL, NB_DEV, 64, 64)
    places_all = pattern.reshape(N_ROW * N_COL, NB_DEV, 2)
    stored_all = counts.reshape(-1)

    def visit(stress_rate, inputs):
        device, kernel_tiles, places, stored = inputs
        my_row = device // N_COL
        my_col = device % N_COL
        row_slot = places[:, 0]
        col_slot = places[:, 1]
        global_row = (my_row * N_COL * per_seg + row_slot).astype(jnp.int32)
        global_col = ((col_slot // per_seg * N_COL + my_col) * per_seg + col_slot % per_seg).astype(jnp.int32)
        active = jnp.arange(NB_DEV, dtype=jnp.int32) < stored
        dense_tiles = kernel_tiles.astype(jnp.float32)
        direct = jnp.einsum('bij,bj->bi', dense_tiles, pieces[global_col], precision=lax.Precision.HIGHEST)
        mirror = jnp.einsum('bij,bi->bj', dense_tiles, pieces[global_row], precision=lax.Precision.HIGHEST)
        direct = jnp.where(active[:, None], direct, 0.0)
        mirror = jnp.where((active & (global_row != global_col))[:, None], mirror, 0.0)
        stress_rate = stress_rate.at[global_row].add(direct).at[global_col].add(mirror)
        return (stress_rate, None)
    start = jnp.zeros(pieces.shape, jnp.float32)
    stress_rate, unused = lax.scan(visit, start, (jnp.arange(N_ROW * N_COL, dtype=jnp.int32), tiles_all, places_all, stored_all))
    return stress_rate.reshape(-1)

def friction_solve(rate_log, stress, state, normal_stress, rate_param, damping):
    for turn_index in range(NEWTON):
        speed = jnp.exp(rate_log)
        ratio = 0.5 * jnp.exp(rate_log + state / rate_param)
        misfit = stress - damping * speed - normal_stress * rate_param * inverse_sinh(ratio)
        slope = -damping * speed - normal_stress * rate_param * ratio / jnp.sqrt(1.0 + ratio * ratio)
        rate_log = rate_log - misfit / slope
    return rate_log

def reference(log_rate, state, excess, normal_stress, rate_param, state_param, slip_length, self_stiffness, damping, blocks, pattern, counts):
    rate_log = log_rate
    balance = normal_stress * rate_param * inverse_sinh(0.5 * jnp.exp(log_rate + state / rate_param)) + damping * jnp.exp(log_rate)
    stress = balance * (1.0 + excess)
    for step_index in range(STEPS):
        speed = jnp.exp(rate_log)
        pushed = (speed - 1.0).astype(jnp.bfloat16)
        stress_rate = apply_kernel(pushed, blocks, pattern, counts)
        new_stress = stress + time_step * (stress_rate - self_stiffness * (speed - 1.0))
        state = state + time_step * (state_param / slip_length) * (jnp.exp(-state / state_param) - speed)
        stress = new_stress
        rate_log = friction_solve(rate_log, stress, state, normal_stress, rate_param, damping)
    return (rate_log, state, stress)
```

```python
import functools

import jax
import jax.numpy as jnp
from jax import lax
from jax.experimental import pallas as pl
from jax.experimental.pallas import tpu as pltpu
from jax.sharding import PartitionSpec as P

STEPS = 2
NEWTON = 4
EDGE = 64
LANES = 128
SPAN = 512
MESH = pl.DeviceIdType.MESH

time_step = 0.25


def inverse_sinh(value):
    return jnp.log(value + jnp.sqrt(1.0 + value * value))


def friction_solve(rate_log, stress, state, normal_stress, rate_param, damping):
    for turn_index in range(NEWTON):
        speed = jnp.exp(rate_log)
        ratio = 0.5 * jnp.exp(rate_log + state / rate_param)
        misfit = stress - damping * speed - normal_stress * rate_param * inverse_sinh(ratio)
        slope = -damping * speed - normal_stress * rate_param * ratio / jnp.sqrt(
            1.0 + ratio * ratio
        )
        rate_log = rate_log - misfit / slope
    return rate_log


def dot(left, right):
    return jnp.dot(left, right, preferred_element_type=jnp.float32)


def twice(pieces):
    count, half, lanes = pieces.shape
    flat = pieces.astype(jnp.float32).reshape(count * half, lanes)
    other = pltpu.roll(flat, EDGE, 1)
    low = lax.broadcasted_iota(jnp.int32, flat.shape, 1) < EDGE
    even = jnp.where(low, flat, other).reshape(count, half, lanes)
    odd = jnp.where(low, other, flat).reshape(count, half, lanes)
    both = jnp.concatenate([even, odd], axis=1)
    return both.reshape(count * 2 * half, lanes).astype(jnp.bfloat16)


def scatter(onehot, values, count, half):
    high = values.astype(jnp.bfloat16)
    rest = values - high.astype(jnp.float32)
    middle = rest.astype(jnp.bfloat16)
    low = (rest - middle.astype(jnp.float32)).astype(jnp.bfloat16)
    sums = dot(onehot, jnp.concatenate([high, middle, low], axis=1))
    sums = sums[:, :LANES] + sums[:, LANES : 2 * LANES] + sums[:, 2 * LANES :]
    sums = sums.reshape(count, 2, half, LANES)
    even, odd = sums[:, 0], sums[:, 1]
    return jnp.where(lax.broadcasted_iota(jnp.int32, even.shape, 2) < EDGE, even, odd)


def body(
    rows,
    cols,
    counts_ref,
    pattern_ref,
    log_rate_ref,
    state_in_ref,
    excess_ref,
    normal_ref,
    rate_param_ref,
    state_param_ref,
    slip_ref,
    stiff_ref,
    damping_ref,
    blocks_ref,
    rate_ref,
    state_ref,
    stress_ref,
    tiles,
    row_pick,
    col_pick,
    row_place,
    col_place,
    spread,
    gather_sum,
    row_tab,
    col_tab,
    row_send,
    col_send,
    row_land,
    col_land,
    tile_sem,
    sems_row_tab,
    sems_col_tab,
    sems_row_part,
    sems_col_part,
):
    my_row = lax.axis_index("row")
    my_col = lax.axis_index("col")
    half = log_rate_ref.shape[0]
    per_seg = 2 * half
    slots, width = tiles.shape
    groups = tile_sem.shape[0]
    depth = slots // groups

    barrier = pltpu.get_barrier_semaphore()
    for k in range(1, cols):
        pl.semaphore_signal(
            barrier, inc=1, device_id={"col": lax.rem(my_col + k, cols)}, device_id_type=MESH
        )
    for k in range(1, rows):
        pl.semaphore_signal(
            barrier, inc=1, device_id={"row": lax.rem(my_row + k, rows)}, device_id_type=MESH
        )

    def tile_copy(group):
        part = pl.ds(group * depth, depth)
        return pltpu.make_async_copy(blocks_ref.at[part], tiles.at[part], tile_sem.at[group])

    for group in range(groups):
        tile_copy(group).start()

    rate_log = log_rate_ref[...]
    state = state_in_ref[...]
    rate_param = rate_param_ref[...]
    balance = normal_ref[...] * rate_param * inverse_sinh(
        0.5 * jnp.exp(rate_log + state / rate_param)
    ) + damping_ref[...] * jnp.exp(rate_log)
    rate_ref[...] = rate_log
    state_ref[...] = state
    stress_ref[...] = balance * (1.0 + excess_ref[...])

    row_slot = pattern_ref[0:1, :]
    col_slot = pattern_ref[1:2, :]
    active = lax.broadcasted_iota(jnp.int32, (1, slots), 1) < counts_ref[0, 0]
    diagonal = (col_slot // per_seg == my_row) & (
        row_slot == my_col * per_seg + col_slot % per_seg
    )

    def position(block):
        inner = block % per_seg
        return (block // per_seg) * per_seg + (inner % 2) * half + inner // 2

    def fill(place, pick, block, keep):
        total = place.shape[0]
        hit = position(block) == lax.broadcasted_iota(jnp.int32, (total, slots), 0)
        ones = jnp.where(hit, 1.0, 0.0)
        pick[...] = ones.T.astype(jnp.bfloat16)
        place[...] = jnp.where(keep, ones, 0.0).astype(jnp.bfloat16)

    fill(row_place, row_pick, row_slot, active)
    fill(col_place, col_pick, col_slot, active & jnp.logical_not(diagonal))
    spread[...] = jnp.where(
        lax.broadcasted_iota(jnp.int32, spread.shape, 0)
        == lax.broadcasted_iota(jnp.int32, spread.shape, 1) // EDGE,
        1.0,
        0.0,
    ).astype(jnp.bfloat16)
    gather_sum[...] = jnp.where(
        lax.broadcasted_iota(jnp.int32, gather_sum.shape, 0) // EDGE
        == lax.broadcasted_iota(jnp.int32, gather_sum.shape, 1) % EDGE,
        1.0,
        0.0,
    ).astype(jnp.bfloat16)

    def tab_copy(step, axis, k, sender):
        tab, sems, me, count = (
            (row_tab, sems_row_tab, my_col, cols)
            if axis == "col"
            else (col_tab, sems_col_tab, my_row, rows)
        )
        slot = me if sender else lax.rem(me - k + count, count)
        return pltpu.make_async_remote_copy(
            src_ref=tab.at[step, slot],
            dst_ref=tab.at[step, slot],
            send_sem=sems.at[0, step, k],
            recv_sem=sems.at[1, step, k],
            device_id={axis: lax.rem(me + k, count)},
            device_id_type=MESH,
        )

    def part_copy(step, axis, k):
        send, land, sems, me, count = (
            (row_send, row_land, sems_row_part, my_col, cols)
            if axis == "col"
            else (col_send, col_land, sems_col_part, my_row, rows)
        )
        target = lax.rem(me + k, count)
        return pltpu.make_async_remote_copy(
            src_ref=send.at[step, target],
            dst_ref=land.at[step, k - 1],
            send_sem=sems.at[0, step, k],
            recv_sem=sems.at[1, step, k],
            device_id={axis: target},
            device_id_type=MESH,
        )

    pl.semaphore_wait(barrier, rows + cols - 2)

    def one_step(step, carry):
        rate_log = rate_ref[...]
        speed = jnp.exp(rate_log)
        pushed = (speed - 1.0).astype(jnp.bfloat16)
        row_tab[step, my_col] = pushed
        col_tab[step, my_row] = pushed
        for k in range(1, rows):
            tab_copy(step, "row", k, True).start()
        for k in range(1, cols):
            tab_copy(step, "col", k, True).start()

        @pl.when(step == 0)
        def _():
            for group in range(groups):
                tile_copy(group).wait()

        for k in range(1, cols):
            tab_copy(step, "col", k, False).wait_recv()
        row_values = dot(row_pick[...], twice(row_tab[step])).astype(jnp.bfloat16)

        def mirror_turn(turn, total):
            part = pl.ds(pl.multiple_of(turn * SPAN, SPAN), SPAN)
            product = tiles[:, part].astype(jnp.float32) * dot(row_values, spread[:, part])
            for c in range(SPAN // LANES):
                total = total + product[:, c * LANES : (c + 1) * LANES]
            return total

        zero = jnp.zeros((slots, LANES), jnp.float32)
        mirror = lax.fori_loop(0, width // SPAN, mirror_turn, zero)
        mirror = mirror + pltpu.roll(mirror, EDGE, 1)
        col_send[step] = scatter(col_place[...], mirror, rows, half)
        for k in range(1, rows):
            part_copy(step, "row", k).start()

        for k in range(1, rows):
            tab_copy(step, "row", k, False).wait_recv()
        col_values = dot(col_pick[...], twice(col_tab[step]))

        def direct_turn(turn, total):
            part = pl.ds(pl.multiple_of(turn * SPAN, SPAN), SPAN)
            product = tiles[:, part].astype(jnp.float32) * jnp.concatenate(
                [col_values] * (SPAN // LANES), axis=1
            )
            high = product.astype(jnp.bfloat16)
            low = (product - high.astype(jnp.float32)).astype(jnp.bfloat16)
            adder = gather_sum[part, :]
            return total + (dot(high, adder) + dot(low, adder))

        direct = lax.fori_loop(0, width // SPAN, direct_turn, zero)
        row_send[step] = scatter(row_place[...], direct, cols, half)
        for k in range(1, cols):
            part_copy(step, "col", k).start()

        state = state_ref[...]
        state_param = state_param_ref[...]
        new_state = state + time_step * (state_param / slip_ref[...]) * (
            jnp.exp(-state / state_param) - speed
        )
        stress_rate = col_send[step, my_row] + row_send[step, my_col]
        for k in range(1, rows):
            part_copy(step, "row", k).wait_recv()
            stress_rate = stress_rate + col_land[step, k - 1]
        for k in range(1, cols):
            part_copy(step, "col", k).wait_recv()
            stress_rate = stress_rate + row_land[step, k - 1]
        stress = stress_ref[...] + time_step * (stress_rate - stiff_ref[...] * (speed - 1.0))
        state_ref[...] = new_state
        stress_ref[...] = stress
        rate_ref[...] = friction_solve(
            rate_log, stress, new_state, normal_ref[...], rate_param_ref[...], damping_ref[...]
        )
        for k in range(1, rows):
            tab_copy(step, "row", k, True).wait_send()
            part_copy(step, "row", k).wait_send()
        for k in range(1, cols):
            tab_copy(step, "col", k, True).wait_send()
            part_copy(step, "col", k).wait_send()
        return carry

    lax.fori_loop(0, STEPS, one_step, 0)


def on_device(*arguments):
    vectors, (blocks, pattern, counts) = arguments[:9], arguments[9:]
    rows = lax.axis_size("row")
    cols = lax.axis_size("col")
    patches = vectors[0].shape[0]
    shape = (patches // LANES, LANES)
    half = shape[0]
    slots, width = blocks.shape[2], blocks.shape[3]
    blocks_row = cols * 2 * half
    blocks_col = rows * 2 * half
    vmem = pl.BlockSpec(memory_space=pltpu.VMEM)
    bf16, f32 = jnp.bfloat16, jnp.float32
    outputs = pl.pallas_call(
        functools.partial(body, rows, cols),
        out_shape=[jax.ShapeDtypeStruct(shape, f32)] * 3,
        in_specs=[pl.BlockSpec(memory_space=pltpu.SMEM)]
        + [vmem] * 10
        + [pl.BlockSpec(memory_space=pl.ANY)],
        out_specs=[vmem] * 3,
        scratch_shapes=[
            pltpu.VMEM((slots, width), bf16),
            pltpu.VMEM((slots, blocks_row), bf16),
            pltpu.VMEM((slots, blocks_col), bf16),
            pltpu.VMEM((blocks_row, slots), bf16),
            pltpu.VMEM((blocks_col, slots), bf16),
            pltpu.VMEM((LANES, width), bf16),
            pltpu.VMEM((width, LANES), bf16),
            pltpu.VMEM((STEPS, cols) + shape, bf16),
            pltpu.VMEM((STEPS, rows) + shape, bf16),
            pltpu.VMEM((STEPS, cols) + shape, f32),
            pltpu.VMEM((STEPS, rows) + shape, f32),
            pltpu.VMEM((STEPS, cols - 1) + shape, f32),
            pltpu.VMEM((STEPS, rows - 1) + shape, f32),
            pltpu.SemaphoreType.DMA((4,)),
            pltpu.SemaphoreType.DMA((2, STEPS, cols)),
            pltpu.SemaphoreType.DMA((2, STEPS, rows)),
            pltpu.SemaphoreType.DMA((2, STEPS, cols)),
            pltpu.SemaphoreType.DMA((2, STEPS, rows)),
        ],
        compiler_params=pltpu.CompilerParams(
            collective_id=0, has_side_effects=True, vmem_limit_bytes=40 * 1024 * 1024
        ),
    )(
        counts,
        pattern.reshape(slots, 2).T,
        *[vector.reshape(shape) for vector in vectors],
        blocks.reshape(slots, width),
    )
    return tuple(output.reshape(patches) for output in outputs)


def solution(mesh):
    patches = P(("row", "col"))
    in_specs = (patches,) * 9 + (
        P("row", "col", None, None),
        P("row", "col", None, None),
        P("row", "col"),
    )
    return jax.shard_map(
        on_device, mesh=mesh, in_specs=in_specs, out_specs=(patches,) * 3, check_vma=False
    )
```

```python
import functools

import jax
import jax.numpy as jnp
from jax import lax
from jax.experimental import pallas as pl
from jax.experimental.pallas import tpu as pltpu
from jax.sharding import PartitionSpec as P

STEPS = 2
NEWTON = 4
EDGE = 64
LANES = 128
SPAN = 512
MESH = pl.DeviceIdType.MESH

time_step = 0.25


def inverse_sinh(value):
    return jnp.log(value + jnp.sqrt(1.0 + value * value))


def friction_solve(rate_log, stress, state, normal_stress, rate_param, damping):
    for turn_index in range(NEWTON):
        speed = jnp.exp(rate_log)
        ratio = 0.5 * jnp.exp(rate_log + state / rate_param)
        misfit = stress - damping * speed - normal_stress * rate_param * inverse_sinh(ratio)
        slope = -damping * speed - normal_stress * rate_param * ratio / jnp.sqrt(
            1.0 + ratio * ratio
        )
        rate_log = rate_log - misfit / slope
    return rate_log


def dot(left, right):
    return jnp.dot(left, right, preferred_element_type=jnp.float32)


def twice(pieces):
    count, half, lanes = pieces.shape
    flat = pieces.astype(jnp.float32).reshape(count * half, lanes)
    other = pltpu.roll(flat, EDGE, 1)
    low = lax.broadcasted_iota(jnp.int32, flat.shape, 1) < EDGE
    even = jnp.where(low, flat, other).reshape(count, half, lanes)
    odd = jnp.where(low, other, flat).reshape(count, half, lanes)
    both = jnp.concatenate([even, odd], axis=1)
    return both.reshape(count * 2 * half, lanes).astype(jnp.bfloat16)


def scatter(onehot, values, count, half):
    high = values.astype(jnp.bfloat16)
    rest = values - high.astype(jnp.float32)
    middle = rest.astype(jnp.bfloat16)
    low = (rest - middle.astype(jnp.float32)).astype(jnp.bfloat16)
    sums = dot(onehot, jnp.concatenate([high, middle, low], axis=1))
    sums = sums[:, :LANES] + sums[:, LANES : 2 * LANES] + sums[:, 2 * LANES :]
    sums = sums.reshape(count, 2, half, LANES)
    even, odd = sums[:, 0], sums[:, 1]
    return jnp.where(lax.broadcasted_iota(jnp.int32, even.shape, 2) < EDGE, even, odd)


def body(
    rows,
    cols,
    counts_ref,
    pattern_hbm,
    log_rate_hbm,
    state_hbm,
    excess_hbm,
    normal_hbm,
    rate_param_hbm,
    state_param_hbm,
    slip_hbm,
    stiff_hbm,
    damping_hbm,
    blocks_ref,
    final_ref,
    inputs,
    pattern_ref,
    tiles,
    row_pick,
    col_pick,
    row_place,
    col_place,
    spread,
    gather_sum,
    row_tab,
    col_tab,
    row_send,
    col_send,
    row_land,
    col_land,
    tile_sem,
    input_sem,
    sems_row_tab,
    sems_col_tab,
    sems_row_part,
    sems_col_part,
):
    my_row = lax.axis_index("row")
    my_col = lax.axis_index("col")
    half = log_rate_hbm.shape[0]
    per_seg = 2 * half
    slots, width = tiles.shape
    groups = tile_sem.shape[0]
    depth = slots // groups

    barrier = pltpu.get_barrier_semaphore()
    for k in range(1, cols):
        pl.semaphore_signal(
            barrier, inc=1, device_id={"col": lax.rem(my_col + k, cols)}, device_id_type=MESH
        )
    for k in range(1, rows):
        pl.semaphore_signal(
            barrier, inc=1, device_id={"row": lax.rem(my_row + k, rows)}, device_id_type=MESH
        )

    def tile_copy(group):
        part = pl.ds(group * depth, depth)
        return pltpu.make_async_copy(blocks_ref.at[part], tiles.at[part], tile_sem.at[group])

    vectors = (
        log_rate_hbm,
        state_hbm,
        excess_hbm,
        normal_hbm,
        rate_param_hbm,
        state_param_hbm,
        slip_hbm,
        stiff_hbm,
        damping_hbm,
    )
    input_copies = [
        pltpu.make_async_copy(vector, inputs.at[index], input_sem.at[index])
        for index, vector in enumerate(vectors)
    ]
    input_copies.append(
        pltpu.make_async_copy(pattern_hbm, pattern_ref, input_sem.at[len(vectors)])
    )
    for copy in input_copies:
        copy.start()
    for group in range(groups):
        tile_copy(group).start()
    for copy in input_copies:
        copy.wait()
    rate_in, state_in, excess_ref, normal_in, rate_param_in = (inputs.at[n] for n in range(5))
    state_param_ref, slip_ref, stiff_ref, damping_in = (inputs.at[n] for n in range(5, 9))
    rate_ref, state_ref, stress_ref, normal_ref, rate_param_ref, damping_ref = (
        final_ref.at[n] for n in range(6)
    )
    normal_ref[...] = normal_in[...]
    rate_param_ref[...] = rate_param_in[...]
    damping_ref[...] = damping_in[...]
    rate_log = rate_in[...]
    state = state_in[...]
    rate_param = rate_param_ref[...]
    balance = normal_ref[...] * rate_param * inverse_sinh(
        0.5 * jnp.exp(rate_log + state / rate_param)
    ) + damping_ref[...] * jnp.exp(rate_log)
    rate_ref[...] = rate_log
    state_ref[...] = state
    stress_ref[...] = balance * (1.0 + excess_ref[...])

    row_slot = pattern_ref[0:1, :]
    col_slot = pattern_ref[1:2, :]
    active = lax.broadcasted_iota(jnp.int32, (1, slots), 1) < counts_ref[0, 0]
    diagonal = (col_slot // per_seg == my_row) & (
        row_slot == my_col * per_seg + col_slot % per_seg
    )

    def position(block):
        inner = block % per_seg
        return (block // per_seg) * per_seg + (inner % 2) * half + inner // 2

    def fill(place, pick, block, keep):
        total = place.shape[0]
        hit = position(block) == lax.broadcasted_iota(jnp.int32, (total, slots), 0)
        ones = jnp.where(hit, 1.0, 0.0)
        pick[...] = ones.T.astype(jnp.bfloat16)
        place[...] = jnp.where(keep, ones, 0.0).astype(jnp.bfloat16)

    fill(row_place, row_pick, row_slot, active)
    fill(col_place, col_pick, col_slot, active & jnp.logical_not(diagonal))
    spread[...] = jnp.where(
        lax.broadcasted_iota(jnp.int32, spread.shape, 0)
        == lax.broadcasted_iota(jnp.int32, spread.shape, 1) // EDGE,
        1.0,
        0.0,
    ).astype(jnp.bfloat16)
    gather_sum[...] = jnp.where(
        lax.broadcasted_iota(jnp.int32, gather_sum.shape, 0) // EDGE
        == lax.broadcasted_iota(jnp.int32, gather_sum.shape, 1) % EDGE,
        1.0,
        0.0,
    ).astype(jnp.bfloat16)

    def tab_copy(step, axis, k, sender):
        tab, sems, me, count = (
            (row_tab, sems_row_tab, my_col, cols)
            if axis == "col"
            else (col_tab, sems_col_tab, my_row, rows)
        )
        slot = me if sender else lax.rem(me - k + count, count)
        return pltpu.make_async_remote_copy(
            src_ref=tab.at[step, slot],
            dst_ref=tab.at[step, slot],
            send_sem=sems.at[0, step, k],
            recv_sem=sems.at[1, step, k],
            device_id={axis: lax.rem(me + k, count)},
            device_id_type=MESH,
        )

    def part_copy(step, axis, k):
        send, land, sems, me, count = (
            (row_send, row_land, sems_row_part, my_col, cols)
            if axis == "col"
            else (col_send, col_land, sems_col_part, my_row, rows)
        )
        target = lax.rem(me + k, count)
        return pltpu.make_async_remote_copy(
            src_ref=send.at[step, target],
            dst_ref=land.at[step, k - 1],
            send_sem=sems.at[0, step, k],
            recv_sem=sems.at[1, step, k],
            device_id={axis: target},
            device_id_type=MESH,
        )

    pl.semaphore_wait(barrier, rows + cols - 2)

    def one_step(step, carry):
        rate_log = rate_ref[...]
        speed = jnp.exp(rate_log)
        pushed = (speed - 1.0).astype(jnp.bfloat16)
        row_tab[step, my_col] = pushed
        col_tab[step, my_row] = pushed
        for k in range(1, rows):
            tab_copy(step, "row", k, True).start()
        for k in range(1, cols):
            tab_copy(step, "col", k, True).start()

        @pl.when(step == 0)
        def _():
            for group in range(groups):
                tile_copy(group).wait()

        for k in range(1, cols):
            tab_copy(step, "col", k, False).wait_recv()
        row_values = dot(row_pick[...], twice(row_tab[step])).astype(jnp.bfloat16)

        def mirror_turn(turn, total):
            part = pl.ds(pl.multiple_of(turn * SPAN, SPAN), SPAN)
            product = tiles[:, part].astype(jnp.float32) * dot(row_values, spread[:, part])
            for c in range(SPAN // LANES):
                total = total + product[:, c * LANES : (c + 1) * LANES]
            return total

        zero = jnp.zeros((slots, LANES), jnp.float32)
        mirror = lax.fori_loop(0, width // SPAN, mirror_turn, zero)
        mirror = mirror + pltpu.roll(mirror, EDGE, 1)
        col_send[step] = scatter(col_place[...], mirror, rows, half)
        for k in range(1, rows):
            part_copy(step, "row", k).start()

        for k in range(1, rows):
            tab_copy(step, "row", k, False).wait_recv()
        col_values = dot(col_pick[...], twice(col_tab[step]))

        def direct_turn(turn, total):
            part = pl.ds(pl.multiple_of(turn * SPAN, SPAN), SPAN)
            product = tiles[:, part].astype(jnp.float32) * jnp.concatenate(
                [col_values] * (SPAN // LANES), axis=1
            )
            high = product.astype(jnp.bfloat16)
            low = (product - high.astype(jnp.float32)).astype(jnp.bfloat16)
            adder = gather_sum[part, :]
            return total + (dot(high, adder) + dot(low, adder))

        direct = lax.fori_loop(0, width // SPAN, direct_turn, zero)
        row_send[step] = scatter(row_place[...], direct, cols, half)
        for k in range(1, cols):
            part_copy(step, "col", k).start()

        state = state_ref[...]
        state_param = state_param_ref[...]
        new_state = state + time_step * (state_param / slip_ref[...]) * (
            jnp.exp(-state / state_param) - speed
        )
        stress_rate = col_send[step, my_row] + row_send[step, my_col]
        for k in range(1, rows):
            part_copy(step, "row", k).wait_recv()
            stress_rate = stress_rate + col_land[step, k - 1]
        for k in range(1, cols):
            part_copy(step, "col", k).wait_recv()
            stress_rate = stress_rate + row_land[step, k - 1]
        stress = stress_ref[...] + time_step * (stress_rate - stiff_ref[...] * (speed - 1.0))
        state_ref[...] = new_state
        stress_ref[...] = stress

        @pl.when(step < STEPS - 1)
        def _():
            rate_ref[...] = friction_solve(
                rate_log, stress, new_state, normal_ref[...], rate_param_ref[...], damping_ref[...]
            )

        for k in range(1, rows):
            tab_copy(step, "row", k, True).wait_send()
            part_copy(step, "row", k).wait_send()
        for k in range(1, cols):
            tab_copy(step, "col", k, True).wait_send()
            part_copy(step, "col", k).wait_send()
        return carry

    lax.fori_loop(0, STEPS, one_step, 0)


def finish(final_ref, rate_ref, state_ref, stress_ref):
    rate_log, state, stress, normal_stress, rate_param, damping = (final_ref[n] for n in range(6))
    state_ref[...] = state
    stress_ref[...] = stress
    rate_ref[...] = friction_solve(rate_log, stress, state, normal_stress, rate_param, damping)


def on_device(*arguments):
    vectors, (blocks, pattern, counts) = arguments[:9], arguments[9:]
    rows = lax.axis_size("row")
    cols = lax.axis_size("col")
    patches = vectors[0].shape[0]
    shape = (patches // LANES, LANES)
    half = shape[0]
    slots, width = blocks.shape[2], blocks.shape[3]
    blocks_row = cols * 2 * half
    blocks_col = rows * 2 * half
    vmem = pl.BlockSpec(memory_space=pltpu.VMEM)
    bf16, f32 = jnp.bfloat16, jnp.float32
    hbm = pl.BlockSpec(memory_space=pltpu.HBM)
    final = pl.pallas_call(
        functools.partial(body, rows, cols),
        out_shape=jax.ShapeDtypeStruct((6,) + shape, f32),
        in_specs=[pl.BlockSpec(memory_space=pltpu.SMEM)] + [hbm] * 11,
        out_specs=vmem,
        scratch_shapes=[
            pltpu.VMEM((9,) + shape, f32),
            pltpu.VMEM((2, slots), jnp.int32),
            pltpu.VMEM((slots, width), bf16),
            pltpu.VMEM((slots, blocks_row), bf16),
            pltpu.VMEM((slots, blocks_col), bf16),
            pltpu.VMEM((blocks_row, slots), bf16),
            pltpu.VMEM((blocks_col, slots), bf16),
            pltpu.VMEM((LANES, width), bf16),
            pltpu.VMEM((width, LANES), bf16),
            pltpu.VMEM((STEPS, cols) + shape, bf16),
            pltpu.VMEM((STEPS, rows) + shape, bf16),
            pltpu.VMEM((STEPS, cols) + shape, f32),
            pltpu.VMEM((STEPS, rows) + shape, f32),
            pltpu.VMEM((STEPS, cols - 1) + shape, f32),
            pltpu.VMEM((STEPS, rows - 1) + shape, f32),
            pltpu.SemaphoreType.DMA((4,)),
            pltpu.SemaphoreType.DMA((10,)),
            pltpu.SemaphoreType.DMA((2, STEPS, cols)),
            pltpu.SemaphoreType.DMA((2, STEPS, rows)),
            pltpu.SemaphoreType.DMA((2, STEPS, cols)),
            pltpu.SemaphoreType.DMA((2, STEPS, rows)),
        ],
        compiler_params=pltpu.CompilerParams(
            collective_id=0, has_side_effects=True, vmem_limit_bytes=60 * 1024 * 1024
        ),
    )(
        counts,
        pattern.reshape(slots, 2).T,
        *[vector.reshape(shape) for vector in vectors],
        blocks.reshape(slots, width),
    )
    outputs = pl.pallas_call(
        finish,
        out_shape=[jax.ShapeDtypeStruct(shape, f32)] * 3,
        in_specs=[vmem],
        out_specs=[vmem] * 3,
    )(final)
    return tuple(output.reshape(patches) for output in outputs)


def solution(mesh):
    patches = P(("row", "col"))
    in_specs = (patches,) * 9 + (
        P("row", "col", None, None),
        P("row", "col", None, None),
        P("row", "col"),
    )
    return jax.shard_map(
        on_device, mesh=mesh, in_specs=in_specs, out_specs=(patches,) * 3, check_vma=False
    )
```

```python
import functools

import jax
import jax.numpy as jnp
from jax import lax
from jax.experimental import pallas as pl
from jax.experimental.pallas import tpu as pltpu
from jax.sharding import PartitionSpec as P

STEPS = 2
NEWTON = 4
EDGE = 64
LANES = 128
SPAN = 512
QUAD = 4
GROUP = LANES // QUAD
MESH = pl.DeviceIdType.MESH

time_step = 0.25


def inverse_sinh(value):
    return jnp.log(value + jnp.sqrt(1.0 + value * value))


def friction_solve(rate_log, stress, state, normal_stress, rate_param, damping):
    for turn_index in range(NEWTON):
        speed = jnp.exp(rate_log)
        ratio = 0.5 * jnp.exp(rate_log + state / rate_param)
        misfit = stress - damping * speed - normal_stress * rate_param * inverse_sinh(ratio)
        slope = -damping * speed - normal_stress * rate_param * ratio / jnp.sqrt(
            1.0 + ratio * ratio
        )
        rate_log = rate_log - misfit / slope
    return rate_log


def dot(left, right):
    return jnp.dot(left, right, preferred_element_type=jnp.float32)


def twice(pieces):
    count, half, lanes = pieces.shape
    flat = pieces.astype(jnp.float32).reshape(count * half, lanes)
    other = pltpu.roll(flat, EDGE, 1)
    low = lax.broadcasted_iota(jnp.int32, flat.shape, 1) < EDGE
    even = jnp.where(low, flat, other).reshape(count, half, lanes)
    odd = jnp.where(low, other, flat).reshape(count, half, lanes)
    both = jnp.concatenate([even, odd], axis=1)
    return both.reshape(count * 2 * half, lanes).astype(jnp.bfloat16)


def three_terms(values):
    high = values.astype(jnp.bfloat16)
    rest = values - high.astype(jnp.float32)
    middle = rest.astype(jnp.bfloat16)
    low = (rest - middle.astype(jnp.float32)).astype(jnp.bfloat16)
    return [high, middle, low]


def scatter(onehot, values):
    sums = dot(onehot, jnp.concatenate(three_terms(values), axis=1))
    return sums[:, :LANES] + sums[:, LANES : 2 * LANES] + sums[:, 2 * LANES :]


def paired(sums, count, half):
    sums = sums.reshape(count, 2, half, LANES)
    even, odd = sums[:, 0], sums[:, 1]
    return jnp.where(lax.broadcasted_iota(jnp.int32, even.shape, 2) < EDGE, even, odd)


def body(
    rows,
    cols,
    counts_ref,
    pattern_hbm,
    log_rate_hbm,
    state_hbm,
    excess_hbm,
    normal_hbm,
    rate_param_hbm,
    state_param_hbm,
    slip_hbm,
    stiff_hbm,
    damping_hbm,
    blocks_ref,
    final_ref,
    inputs,
    pattern_ref,
    tiles,
    row_pick,
    col_find,
    col_place,
    spread,
    weights,
    picked,
    turned,
    row_tab,
    col_tab,
    row_send,
    col_send,
    row_land,
    col_land,
    tile_sem,
    input_sem,
    sems_row_tab,
    sems_col_tab,
    sems_row_part,
    sems_col_part,
):
    my_row = lax.axis_index("row")
    my_col = lax.axis_index("col")
    half = log_rate_hbm.shape[0]
    per_seg = 2 * half
    slots, width = tiles.shape
    groups = tile_sem.shape[0]
    depth = slots // groups

    barrier = pltpu.get_barrier_semaphore()
    for k in range(1, cols):
        pl.semaphore_signal(
            barrier, inc=1, device_id={"col": lax.rem(my_col + k, cols)}, device_id_type=MESH
        )
    for k in range(1, rows):
        pl.semaphore_signal(
            barrier, inc=1, device_id={"row": lax.rem(my_row + k, rows)}, device_id_type=MESH
        )

    def tile_copy(group):
        part = pl.ds(group * depth, depth)
        return pltpu.make_async_copy(blocks_ref.at[part], tiles.at[part], tile_sem.at[group])

    vectors = (
        log_rate_hbm,
        state_hbm,
        excess_hbm,
        normal_hbm,
        rate_param_hbm,
        state_param_hbm,
        slip_hbm,
        stiff_hbm,
        damping_hbm,
    )
    input_copies = [
        pltpu.make_async_copy(vector, inputs.at[index], input_sem.at[index])
        for index, vector in enumerate(vectors)
    ]
    input_copies.append(
        pltpu.make_async_copy(pattern_hbm, pattern_ref, input_sem.at[len(vectors)])
    )
    for copy in input_copies:
        copy.start()
    for group in range(groups):
        tile_copy(group).start()
    for copy in input_copies:
        copy.wait()
    rate_in, state_in, excess_ref, normal_in, rate_param_in = (inputs.at[n] for n in range(5))
    state_param_ref, slip_ref, stiff_ref, damping_in = (inputs.at[n] for n in range(5, 9))
    rate_ref, state_ref, stress_ref, normal_ref, rate_param_ref, damping_ref = (
        final_ref.at[n] for n in range(6)
    )
    normal_ref[...] = normal_in[...]
    rate_param_ref[...] = rate_param_in[...]
    damping_ref[...] = damping_in[...]
    rate_log = rate_in[...]
    state = state_in[...]
    rate_param = rate_param_ref[...]
    balance = normal_ref[...] * rate_param * inverse_sinh(
        0.5 * jnp.exp(rate_log + state / rate_param)
    ) + damping_ref[...] * jnp.exp(rate_log)
    rate_ref[...] = rate_log
    state_ref[...] = state
    stress_ref[...] = balance * (1.0 + excess_ref[...])

    row_slot = pattern_ref[0:1, :]
    col_slot = pattern_ref[1:2, :]
    active = lax.broadcasted_iota(jnp.int32, (1, slots), 1) < counts_ref[0, 0]
    diagonal = (col_slot // per_seg == my_row) & (
        row_slot == my_col * per_seg + col_slot % per_seg
    )

    def position(block):
        inner = block % per_seg
        return (block // per_seg) * per_seg + (inner % 2) * half + inner // 2

    def onehot(block, total):
        hit = position(block) == lax.broadcasted_iota(jnp.int32, (total, slots), 0)
        return jnp.where(hit & active, 1.0, 0.0)

    row_pick[...] = onehot(row_slot, row_pick.shape[1]).T.astype(jnp.bfloat16)
    found = onehot(col_slot, col_place.shape[0])
    col_find[...] = found.astype(jnp.bfloat16)
    col_place[...] = jnp.where(diagonal, 0.0, found).astype(jnp.bfloat16)
    spread[...] = jnp.where(
        lax.broadcasted_iota(jnp.int32, spread.shape, 0)
        == lax.broadcasted_iota(jnp.int32, spread.shape, 1) // EDGE,
        1.0,
        0.0,
    ).astype(jnp.bfloat16)
    def tab_copy(step, axis, k, sender):
        tab, sems, me, count = (
            (row_tab, sems_row_tab, my_col, cols)
            if axis == "col"
            else (col_tab, sems_col_tab, my_row, rows)
        )
        slot = me if sender else lax.rem(me - k + count, count)
        return pltpu.make_async_remote_copy(
            src_ref=tab.at[step, slot],
            dst_ref=tab.at[step, slot],
            send_sem=sems.at[0, step, k],
            recv_sem=sems.at[1, step, k],
            device_id={axis: lax.rem(me + k, count)},
            device_id_type=MESH,
        )

    def part_copy(step, axis, k):
        send, land, sems, me, count = (
            (row_send, row_land, sems_row_part, my_col, cols)
            if axis == "col"
            else (col_send, col_land, sems_col_part, my_row, rows)
        )
        target = lax.rem(me + k, count)
        return pltpu.make_async_remote_copy(
            src_ref=send.at[step, target],
            dst_ref=land.at[step, k - 1],
            send_sem=sems.at[0, step, k],
            recv_sem=sems.at[1, step, k],
            device_id={axis: target},
            device_id_type=MESH,
        )

    pl.semaphore_wait(barrier, rows + cols - 2)

    def one_step(step, carry):
        rate_log = rate_ref[...]
        speed = jnp.exp(rate_log)
        pushed = (speed - 1.0).astype(jnp.bfloat16)
        row_tab[step, my_col] = pushed
        col_tab[step, my_row] = pushed
        for k in range(1, rows):
            tab_copy(step, "row", k, True).start()
        for k in range(1, cols):
            tab_copy(step, "col", k, True).start()

        @pl.when(step == 0)
        def _():
            for group in range(groups):
                tile_copy(group).wait()

        for k in range(1, cols):
            tab_copy(step, "col", k, False).wait_recv()
        row_values = dot(row_pick[...], twice(row_tab[step])).astype(jnp.bfloat16)

        def mirror_turn(turn, total):
            part = pl.ds(pl.multiple_of(turn * SPAN, SPAN), SPAN)
            product = tiles[:, part].astype(jnp.float32) * dot(row_values, spread[:, part])
            for c in range(SPAN // LANES):
                total = total + product[:, c * LANES : (c + 1) * LANES]
            return total

        zero = jnp.zeros((slots, LANES), jnp.float32)
        mirror = lax.fori_loop(0, width // SPAN, mirror_turn, zero)
        mirror = mirror + pltpu.roll(mirror, EDGE, 1)
        col_send[step] = paired(scatter(col_place[...], mirror), rows, half)
        for k in range(1, rows):
            part_copy(step, "row", k).start()

        for k in range(1, rows):
            tab_copy(step, "row", k, False).wait_recv()
        values = lax.dot_general(
            twice(col_tab[step]),
            col_find[...],
            (((0,), (0,)), ((), ())),
            preferred_element_type=jnp.float32,
        )[:EDGE]
        section = lax.broadcasted_iota(jnp.int32, (EDGE, LANES), 1) // GROUP
        for base in range(slots // LANES):
            part = values[:, base * LANES : (base + 1) * LANES]
            shifted = [part] + [pltpu.roll(part, n * GROUP, 1) for n in range(1, QUAD)]
            for inner in range(QUAD):
                weights[base * QUAD + inner] = jnp.concatenate(
                    [
                        jnp.where(section == q, shifted[(q - inner) % QUAD], 0.0)
                        for q in range(QUAD)
                    ],
                    axis=0,
                ).astype(jnp.bfloat16)

        own = lax.broadcasted_iota(jnp.int32, (1, GROUP, LANES), 1) == (
            lax.broadcasted_iota(jnp.int32, (1, GROUP, LANES), 2) % GROUP
        )
        wide = QUAD * EDGE
        fours = width // wide

        def direct_turn(group, carry):
            part = tiles[pl.ds(pl.multiple_of(group * GROUP, GROUP), GROUP), :]
            stacked = jnp.concatenate(
                [part[:, n * wide : (n + 1) * wide] for n in range(fours)], axis=0
            )
            product = dot(stacked, weights[group]).reshape(fours, GROUP, LANES)
            picked[group] = jnp.sum(jnp.where(own, product, 0.0), axis=1)
            return carry

        lax.fori_loop(0, slots // GROUP, direct_turn, 0)
        narrow = lax.broadcasted_iota(jnp.int32, (fours, LANES), 1) // GROUP
        pieces = [[] for q in range(QUAD)]
        for base in range(slots // LANES):
            parts = [picked[base * QUAD + inner] for inner in range(QUAD)]
            for q in range(QUAD):
                joined = jnp.zeros((fours, LANES), jnp.float32)
                for inner in range(QUAD):
                    shift = (inner - q) % QUAD * GROUP
                    moved = pltpu.roll(parts[inner], shift, 1) if shift else parts[inner]
                    joined = jnp.where(narrow == inner, moved, joined)
                pieces[q].append(joined)
        direct = jnp.concatenate([jnp.concatenate(part, axis=1) for part in pieces], axis=0)
        sums = dot(jnp.concatenate(three_terms(direct), axis=0), row_pick[...])
        sums = sums[:EDGE] + sums[EDGE : 2 * EDGE] + sums[2 * EDGE :]
        for q in range(QUAD):
            for copied in range(LANES // EDGE):
                for chunk in range(turned.shape[0]):
                    turned[chunk, pl.ds(copied * EDGE + q, fours, QUAD), :] = sums[
                        q * fours : (q + 1) * fours, chunk * LANES : (chunk + 1) * LANES
                    ]
        back = jnp.concatenate([turned[chunk].T for chunk in range(turned.shape[0])], axis=0)
        row_send[step] = paired(back, cols, half)
        for k in range(1, cols):
            part_copy(step, "col", k).start()

        state = state_ref[...]
        state_param = state_param_ref[...]
        new_state = state + time_step * (state_param / slip_ref[...]) * (
            jnp.exp(-state / state_param) - speed
        )
        stress_rate = col_send[step, my_row] + row_send[step, my_col]
        for k in range(1, rows):
            part_copy(step, "row", k).wait_recv()
            stress_rate = stress_rate + col_land[step, k - 1]
        for k in range(1, cols):
            part_copy(step, "col", k).wait_recv()
            stress_rate = stress_rate + row_land[step, k - 1]
        stress = stress_ref[...] + time_step * (stress_rate - stiff_ref[...] * (speed - 1.0))
        state_ref[...] = new_state
        stress_ref[...] = stress

        @pl.when(step < STEPS - 1)
        def _():
            rate_ref[...] = friction_solve(
                rate_log, stress, new_state, normal_ref[...], rate_param_ref[...], damping_ref[...]
            )

        for k in range(1, rows):
            tab_copy(step, "row", k, True).wait_send()
            part_copy(step, "row", k).wait_send()
        for k in range(1, cols):
            tab_copy(step, "col", k, True).wait_send()
            part_copy(step, "col", k).wait_send()
        return carry

    lax.fori_loop(0, STEPS, one_step, 0)


def finish(final_ref, rate_ref, state_ref, stress_ref):
    rate_log, state, stress, normal_stress, rate_param, damping = (final_ref[n] for n in range(6))
    state_ref[...] = state
    stress_ref[...] = stress
    rate_ref[...] = friction_solve(rate_log, stress, state, normal_stress, rate_param, damping)


def on_device(*arguments):
    vectors, (blocks, pattern, counts) = arguments[:9], arguments[9:]
    rows = lax.axis_size("row")
    cols = lax.axis_size("col")
    patches = vectors[0].shape[0]
    shape = (patches // LANES, LANES)
    half = shape[0]
    slots, width = blocks.shape[2], blocks.shape[3]
    blocks_row = cols * 2 * half
    blocks_col = rows * 2 * half
    vmem = pl.BlockSpec(memory_space=pltpu.VMEM)
    bf16, f32 = jnp.bfloat16, jnp.float32
    hbm = pl.BlockSpec(memory_space=pltpu.HBM)
    final = pl.pallas_call(
        functools.partial(body, rows, cols),
        out_shape=jax.ShapeDtypeStruct((6,) + shape, f32),
        in_specs=[pl.BlockSpec(memory_space=pltpu.SMEM)] + [hbm] * 11,
        out_specs=vmem,
        scratch_shapes=[
            pltpu.VMEM((9,) + shape, f32),
            pltpu.VMEM((2, slots), jnp.int32),
            pltpu.VMEM((slots, width), bf16),
            pltpu.VMEM((slots, blocks_row), bf16),
            pltpu.VMEM((blocks_col, slots), bf16),
            pltpu.VMEM((blocks_col, slots), bf16),
            pltpu.VMEM((LANES, width), bf16),
            pltpu.VMEM((slots // GROUP, QUAD * EDGE, LANES), bf16),
            pltpu.VMEM((slots // GROUP, width // (QUAD * EDGE), LANES), f32),
            pltpu.VMEM((blocks_row // LANES, LANES, LANES), f32),
            pltpu.VMEM((STEPS, cols) + shape, bf16),
            pltpu.VMEM((STEPS, rows) + shape, bf16),
            pltpu.VMEM((STEPS, cols) + shape, f32),
            pltpu.VMEM((STEPS, rows) + shape, f32),
            pltpu.VMEM((STEPS, cols - 1) + shape, f32),
            pltpu.VMEM((STEPS, rows - 1) + shape, f32),
            pltpu.SemaphoreType.DMA((4,)),
            pltpu.SemaphoreType.DMA((10,)),
            pltpu.SemaphoreType.DMA((2, STEPS, cols)),
            pltpu.SemaphoreType.DMA((2, STEPS, rows)),
            pltpu.SemaphoreType.DMA((2, STEPS, cols)),
            pltpu.SemaphoreType.DMA((2, STEPS, rows)),
        ],
        compiler_params=pltpu.CompilerParams(
            collective_id=0, has_side_effects=True, vmem_limit_bytes=60 * 1024 * 1024
        ),
    )(
        counts,
        pattern.reshape(slots, 2).T,
        *[vector.reshape(shape) for vector in vectors],
        blocks.reshape(slots, width),
    )
    outputs = pl.pallas_call(
        finish,
        out_shape=[jax.ShapeDtypeStruct(shape, f32)] * 3,
        in_specs=[vmem],
        out_specs=[vmem] * 3,
    )(final)
    return tuple(output.reshape(patches) for output in outputs)


def solution(mesh):
    patches = P(("row", "col"))
    in_specs = (patches,) * 9 + (
        P("row", "col", None, None),
        P("row", "col", None, None),
        P("row", "col"),
    )
    return jax.shard_map(
        on_device, mesh=mesh, in_specs=in_specs, out_specs=(patches,) * 3, check_vma=False
    )
```

```python
import functools

import jax
import jax.numpy as jnp
from jax import lax
from jax.experimental import pallas as pl
from jax.experimental.pallas import tpu as pltpu
from jax.sharding import PartitionSpec as P

STEPS = 2
NEWTON = 4
EDGE = 64
LANES = 128
SPAN = 256
STRIP = 128
QUAD = 4
GROUP = LANES // QUAD
MESH = pl.DeviceIdType.MESH

time_step = 0.25


def inverse_sinh(value):
    return jnp.log(value + jnp.sqrt(1.0 + value * value))


def friction_solve(rate_log, stress, state, normal_stress, rate_param, damping):
    for turn_index in range(NEWTON):
        speed = jnp.exp(rate_log)
        ratio = 0.5 * jnp.exp(rate_log + state / rate_param)
        misfit = stress - damping * speed - normal_stress * rate_param * inverse_sinh(ratio)
        slope = -damping * speed - normal_stress * rate_param * ratio / jnp.sqrt(
            1.0 + ratio * ratio
        )
        rate_log = rate_log - misfit / slope
    return rate_log


def dot(left, right):
    return jnp.dot(left, right, preferred_element_type=jnp.float32)


def twice(pieces):
    count, half, lanes = pieces.shape
    flat = pieces.astype(jnp.float32).reshape(count * half, lanes)
    other = pltpu.roll(flat, EDGE, 1)
    low = lax.broadcasted_iota(jnp.int32, flat.shape, 1) < EDGE
    even = jnp.where(low, flat, other).reshape(count, half, lanes)
    odd = jnp.where(low, other, flat).reshape(count, half, lanes)
    both = jnp.concatenate([even, odd], axis=1)
    return both.reshape(count * 2 * half, lanes).astype(jnp.bfloat16)


def three_terms(values):
    high = values.astype(jnp.bfloat16)
    rest = values - high.astype(jnp.float32)
    middle = rest.astype(jnp.bfloat16)
    low = (rest - middle.astype(jnp.float32)).astype(jnp.bfloat16)
    return [high, middle, low]


def scatter(onehot, values):
    sums = dot(onehot, jnp.concatenate(three_terms(values), axis=1))
    return sums[:, :LANES] + sums[:, LANES : 2 * LANES] + sums[:, 2 * LANES :]


def paired(sums, count, half):
    sums = sums.reshape(count, 2, half, LANES)
    even, odd = sums[:, 0], sums[:, 1]
    return jnp.where(lax.broadcasted_iota(jnp.int32, even.shape, 2) < EDGE, even, odd)


def body(
    rows,
    cols,
    counts_ref,
    pattern_hbm,
    log_rate_hbm,
    state_hbm,
    excess_hbm,
    normal_hbm,
    rate_param_hbm,
    state_param_hbm,
    slip_hbm,
    stiff_hbm,
    damping_hbm,
    blocks_ref,
    final_ref,
    inputs,
    pattern_ref,
    tiles,
    row_pick,
    col_find,
    col_place,
    spread,
    spread_in,
    mirrored,
    weights,
    picked,
    turned,
    row_tab,
    col_tab,
    row_send,
    col_send,
    row_land,
    col_land,
    tile_sem,
    input_sem,
    sems_row_tab,
    sems_col_tab,
    sems_row_part,
    sems_col_part,
):
    my_row = lax.axis_index("row")
    my_col = lax.axis_index("col")
    half = log_rate_hbm.shape[0]
    per_seg = 2 * half
    slots, width = tiles.shape
    groups = tile_sem.shape[0]
    depth = slots // groups

    barrier = pltpu.get_barrier_semaphore()
    for k in range(1, cols):
        pl.semaphore_signal(
            barrier, inc=1, device_id={"col": lax.rem(my_col + k, cols)}, device_id_type=MESH
        )
    for k in range(1, rows):
        pl.semaphore_signal(
            barrier, inc=1, device_id={"row": lax.rem(my_row + k, rows)}, device_id_type=MESH
        )

    def tile_copy(group):
        part = pl.ds(group * depth, depth)
        return pltpu.make_async_copy(blocks_ref.at[part], tiles.at[part], tile_sem.at[group])

    vectors = (
        log_rate_hbm,
        state_hbm,
        excess_hbm,
        normal_hbm,
        rate_param_hbm,
        state_param_hbm,
        slip_hbm,
        stiff_hbm,
        damping_hbm,
    )
    input_copies = [
        pltpu.make_async_copy(vector, inputs.at[index], input_sem.at[index])
        for index, vector in enumerate(vectors)
    ]
    input_copies.append(
        pltpu.make_async_copy(pattern_hbm, pattern_ref, input_sem.at[len(vectors)])
    )
    for copy in input_copies:
        copy.start()
    for group in range(groups):
        tile_copy(group).start()
    for copy in input_copies:
        copy.wait()
    rate_in, state_in, excess_ref, normal_in, rate_param_in = (inputs.at[n] for n in range(5))
    state_param_ref, slip_ref, stiff_ref, damping_in = (inputs.at[n] for n in range(5, 9))
    rate_ref, state_ref, stress_ref, normal_ref, rate_param_ref, damping_ref = (
        final_ref.at[n] for n in range(6)
    )
    rate_ref[...] = rate_in[...]

    row_slot = pattern_ref[0:1, :]
    col_slot = pattern_ref[1:2, :]
    active = lax.broadcasted_iota(jnp.int32, (1, slots), 1) < counts_ref[0, 0]
    diagonal = (col_slot // per_seg == my_row) & (
        row_slot == my_col * per_seg + col_slot % per_seg
    )

    def position(block):
        inner = block % per_seg
        return (block // per_seg) * per_seg + (inner % 2) * half + inner // 2

    def onehot(block, total):
        hit = position(block) == lax.broadcasted_iota(jnp.int32, (total, slots), 0)
        return jnp.where(hit & active, 1.0, 0.0)

    spread[...] = jnp.where(
        lax.broadcasted_iota(jnp.int32, spread.shape, 0)
        == lax.broadcasted_iota(jnp.int32, spread.shape, 1) // EDGE,
        1.0,
        0.0,
    ).astype(jnp.bfloat16)
    def tab_copy(step, axis, k, sender):
        tab, sems, me, count = (
            (row_tab, sems_row_tab, my_col, cols)
            if axis == "col"
            else (col_tab, sems_col_tab, my_row, rows)
        )
        slot = me if sender else lax.rem(me - k + count, count)
        return pltpu.make_async_remote_copy(
            src_ref=tab.at[step, slot],
            dst_ref=tab.at[step, slot],
            send_sem=sems.at[0, step, k],
            recv_sem=sems.at[1, step, k],
            device_id={axis: lax.rem(me + k, count)},
            device_id_type=MESH,
        )

    def part_copy(step, axis, k):
        send, land, sems, me, count = (
            (row_send, row_land, sems_row_part, my_col, cols)
            if axis == "col"
            else (col_send, col_land, sems_col_part, my_row, rows)
        )
        target = lax.rem(me + k, count)
        return pltpu.make_async_remote_copy(
            src_ref=send.at[step, target],
            dst_ref=land.at[step, k - 1],
            send_sem=sems.at[0, step, k],
            recv_sem=sems.at[1, step, k],
            device_id={axis: target},
            device_id_type=MESH,
        )

    pl.semaphore_wait(barrier, rows + cols - 2)

    def one_step(step, carry):
        rate_log = rate_ref[...]
        speed = jnp.exp(rate_log)
        pushed = (speed - 1.0).astype(jnp.bfloat16)
        row_tab[step, my_col] = pushed
        col_tab[step, my_row] = pushed
        for k in range(1, rows):
            tab_copy(step, "row", k, True).start()
        for k in range(1, cols):
            tab_copy(step, "col", k, True).start()

        @pl.when(step == 0)
        def _():
            normal_ref[...] = normal_in[...]
            rate_param_ref[...] = rate_param_in[...]
            damping_ref[...] = damping_in[...]
            rate_log = rate_in[...]
            state = state_in[...]
            rate_param = rate_param_ref[...]
            balance = normal_ref[...] * rate_param * inverse_sinh(
                0.5 * jnp.exp(rate_log + state / rate_param)
            ) + damping_ref[...] * jnp.exp(rate_log)
            state_ref[...] = state
            stress_ref[...] = balance * (1.0 + excess_ref[...])
            row_pick[...] = onehot(row_slot, row_pick.shape[1]).T.astype(jnp.bfloat16)
            found = onehot(col_slot, col_place.shape[0])
            col_find[...] = found.astype(jnp.bfloat16)
            col_place[...] = jnp.where(diagonal, 0.0, found).astype(jnp.bfloat16)
            for group in range(groups):
                tile_copy(group).wait()

        for k in range(1, cols):
            tab_copy(step, "col", k, False).wait_recv()
        row_values = dot(row_pick[...], twice(row_tab[step])).astype(jnp.bfloat16)

        def mirror_turn(turn, carry):
            strip = pl.ds(pl.multiple_of(turn * STRIP, STRIP), STRIP)
            values = spread_in[strip, :]
            total = jnp.zeros((STRIP, LANES), jnp.float32)
            for begin in range(0, width, SPAN):
                part = pl.ds(begin, SPAN)
                product = tiles[strip, part].astype(jnp.float32) * dot(values, spread[:, part])
                for c in range(SPAN // LANES):
                    total = total + product[:, c * LANES : (c + 1) * LANES]
            mirrored[strip, :] = total
            return carry

        spread_in[...] = row_values
        lax.fori_loop(0, slots // STRIP, mirror_turn, 0)
        mirror = mirrored[...]
        mirror = mirror + pltpu.roll(mirror, EDGE, 1)
        col_send[step] = paired(scatter(col_place[...], mirror), rows, half)
        for k in range(1, rows):
            part_copy(step, "row", k).start()

        for k in range(1, rows):
            tab_copy(step, "row", k, False).wait_recv()
        values = lax.dot_general(
            twice(col_tab[step]),
            col_find[...],
            (((0,), (0,)), ((), ())),
            preferred_element_type=jnp.float32,
        )[:EDGE]
        section = lax.broadcasted_iota(jnp.int32, (EDGE, LANES), 1) // GROUP
        for base in range(slots // LANES):
            part = values[:, base * LANES : (base + 1) * LANES]
            shifted = [part] + [pltpu.roll(part, n * GROUP, 1) for n in range(1, QUAD)]
            for inner in range(QUAD):
                weights[base * QUAD + inner] = jnp.concatenate(
                    [
                        jnp.where(section == q, shifted[(q - inner) % QUAD], 0.0)
                        for q in range(QUAD)
                    ],
                    axis=0,
                ).astype(jnp.bfloat16)

        own = lax.broadcasted_iota(jnp.int32, (1, GROUP, LANES), 1) == (
            lax.broadcasted_iota(jnp.int32, (1, GROUP, LANES), 2) % GROUP
        )
        wide = QUAD * EDGE
        fours = width // wide

        def direct_turn(turn, carry):
            for inner in range(QUAD):
                group = turn * QUAD + inner
                part = tiles[pl.ds(pl.multiple_of(group * GROUP, GROUP), GROUP), :]
                stacked = jnp.concatenate(
                    [part[:, n * wide : (n + 1) * wide] for n in range(fours)], axis=0
                )
                product = dot(stacked, weights[group]).reshape(fours, GROUP, LANES)
                picked[group] = jnp.sum(jnp.where(own, product, 0.0), axis=1)
            return carry

        lax.fori_loop(0, slots // LANES, direct_turn, 0)
        narrow = lax.broadcasted_iota(jnp.int32, (fours, LANES), 1) // GROUP
        pieces = [[] for q in range(QUAD)]
        for base in range(slots // LANES):
            parts = [picked[base * QUAD + inner] for inner in range(QUAD)]
            for q in range(QUAD):
                joined = jnp.zeros((fours, LANES), jnp.float32)
                for inner in range(QUAD):
                    shift = (inner - q) % QUAD * GROUP
                    moved = pltpu.roll(parts[inner], shift, 1) if shift else parts[inner]
                    joined = jnp.where(narrow == inner, moved, joined)
                pieces[q].append(joined)
        direct = jnp.concatenate([jnp.concatenate(part, axis=1) for part in pieces], axis=0)
        sums = dot(jnp.concatenate(three_terms(direct), axis=0), row_pick[...])
        sums = sums[:EDGE] + sums[EDGE : 2 * EDGE] + sums[2 * EDGE :]
        for q in range(QUAD):
            for copied in range(LANES // EDGE):
                for chunk in range(turned.shape[0]):
                    turned[chunk, pl.ds(copied * EDGE + q, fours, QUAD), :] = sums[
                        q * fours : (q + 1) * fours, chunk * LANES : (chunk + 1) * LANES
                    ]
        back = jnp.concatenate([turned[chunk].T for chunk in range(turned.shape[0])], axis=0)
        row_send[step] = paired(back, cols, half)
        for k in range(1, cols):
            part_copy(step, "col", k).start()

        state = state_ref[...]
        state_param = state_param_ref[...]
        new_state = state + time_step * (state_param / slip_ref[...]) * (
            jnp.exp(-state / state_param) - speed
        )
        stress_rate = col_send[step, my_row] + row_send[step, my_col]
        for k in range(1, rows):
            part_copy(step, "row", k).wait_recv()
            stress_rate = stress_rate + col_land[step, k - 1]
        for k in range(1, cols):
            part_copy(step, "col", k).wait_recv()
            stress_rate = stress_rate + row_land[step, k - 1]
        stress = stress_ref[...] + time_step * (stress_rate - stiff_ref[...] * (speed - 1.0))
        state_ref[...] = new_state
        stress_ref[...] = stress

        @pl.when(step < STEPS - 1)
        def _():
            rate_ref[...] = friction_solve(
                rate_log, stress, new_state, normal_ref[...], rate_param_ref[...], damping_ref[...]
            )

        for k in range(1, rows):
            tab_copy(step, "row", k, True).wait_send()
            part_copy(step, "row", k).wait_send()
        for k in range(1, cols):
            tab_copy(step, "col", k, True).wait_send()
            part_copy(step, "col", k).wait_send()
        return carry

    lax.fori_loop(0, STEPS, one_step, 0)


def finish(final_ref, rate_ref, state_ref, stress_ref):
    rate_log, state, stress, normal_stress, rate_param, damping = (final_ref[n] for n in range(6))
    state_ref[...] = state
    stress_ref[...] = stress
    rate_ref[...] = friction_solve(rate_log, stress, state, normal_stress, rate_param, damping)


def on_device(*arguments):
    vectors, (blocks, pattern, counts) = arguments[:9], arguments[9:]
    rows = lax.axis_size("row")
    cols = lax.axis_size("col")
    patches = vectors[0].shape[0]
    shape = (patches // LANES, LANES)
    half = shape[0]
    slots, width = blocks.shape[2], blocks.shape[3]
    blocks_row = cols * 2 * half
    blocks_col = rows * 2 * half
    vmem = pl.BlockSpec(memory_space=pltpu.VMEM)
    bf16, f32 = jnp.bfloat16, jnp.float32
    hbm = pl.BlockSpec(memory_space=pltpu.HBM)
    final = pl.pallas_call(
        functools.partial(body, rows, cols),
        out_shape=jax.ShapeDtypeStruct((6,) + shape, f32),
        in_specs=[pl.BlockSpec(memory_space=pltpu.SMEM)] + [hbm] * 11,
        out_specs=vmem,
        scratch_shapes=[
            pltpu.VMEM((9,) + shape, f32),
            pltpu.VMEM((2, slots), jnp.int32),
            pltpu.VMEM((slots, width), bf16),
            pltpu.VMEM((slots, blocks_row), bf16),
            pltpu.VMEM((blocks_col, slots), bf16),
            pltpu.VMEM((blocks_col, slots), bf16),
            pltpu.VMEM((LANES, width), bf16),
            pltpu.VMEM((slots, LANES), bf16),
            pltpu.VMEM((slots, LANES), f32),
            pltpu.VMEM((slots // GROUP, QUAD * EDGE, LANES), bf16),
            pltpu.VMEM((slots // GROUP, width // (QUAD * EDGE), LANES), f32),
            pltpu.VMEM((blocks_row // LANES, LANES, LANES), f32),
            pltpu.VMEM((STEPS, cols) + shape, bf16),
            pltpu.VMEM((STEPS, rows) + shape, bf16),
            pltpu.VMEM((STEPS, cols) + shape, f32),
            pltpu.VMEM((STEPS, rows) + shape, f32),
            pltpu.VMEM((STEPS, cols - 1) + shape, f32),
            pltpu.VMEM((STEPS, rows - 1) + shape, f32),
            pltpu.SemaphoreType.DMA((4,)),
            pltpu.SemaphoreType.DMA((10,)),
            pltpu.SemaphoreType.DMA((2, STEPS, cols)),
            pltpu.SemaphoreType.DMA((2, STEPS, rows)),
            pltpu.SemaphoreType.DMA((2, STEPS, cols)),
            pltpu.SemaphoreType.DMA((2, STEPS, rows)),
        ],
        compiler_params=pltpu.CompilerParams(
            collective_id=0, has_side_effects=True, vmem_limit_bytes=60 * 1024 * 1024
        ),
    )(
        counts,
        pattern.reshape(slots, 2).T,
        *[vector.reshape(shape) for vector in vectors],
        blocks.reshape(slots, width),
    )
    outputs = pl.pallas_call(
        finish,
        out_shape=[jax.ShapeDtypeStruct(shape, f32)] * 3,
        in_specs=[vmem],
        out_specs=[vmem] * 3,
    )(final)
    return tuple(output.reshape(patches) for output in outputs)


def solution(mesh):
    patches = P(("row", "col"))
    in_specs = (patches,) * 9 + (
        P("row", "col", None, None),
        P("row", "col", None, None),
        P("row", "col"),
    )
    return jax.shard_map(
        on_device, mesh=mesh, in_specs=in_specs, out_specs=(patches,) * 3, check_vma=False
    )
```

```python
import functools

import jax
import jax.numpy as jnp
from jax import lax
from jax.experimental import pallas as pl
from jax.experimental.pallas import tpu as pltpu
from jax.sharding import PartitionSpec as P

STEPS = 2
NEWTON = 4
EDGE = 64
LANES = 128
SPAN = 256
STRIP = 256
BATCH = 8
QUAD = 4
GROUP = LANES // QUAD
MESH = pl.DeviceIdType.MESH

time_step = 0.25


def inverse_sinh(value):
    return jnp.log(value + jnp.sqrt(1.0 + value * value))


def resistance(rate_log, state, normal_stress, rate_param, damping):
    speed = jnp.exp(rate_log)
    ratio = 0.5 * jnp.exp(rate_log + state / rate_param)
    slope = -damping * speed - normal_stress * rate_param * ratio / jnp.sqrt(1.0 + ratio * ratio)
    return damping * speed, normal_stress * rate_param * inverse_sinh(ratio), slope


def friction_solve(rate_log, stress, state, normal_stress, rate_param, damping):
    for turn_index in range(NEWTON - 1):
        viscous, friction, slope = resistance(rate_log, state, normal_stress, rate_param, damping)
        rate_log = rate_log - (stress - viscous - friction) / slope
    return rate_log


def dot(left, right):
    return jnp.dot(left, right, preferred_element_type=jnp.float32)


def twice(pieces):
    count, half, lanes = pieces.shape
    flat = pieces.astype(jnp.float32).reshape(count * half, lanes)
    other = pltpu.roll(flat, EDGE, 1)
    low = lax.broadcasted_iota(jnp.int32, flat.shape, 1) < EDGE
    even = jnp.where(low, flat, other).reshape(count, half, lanes)
    odd = jnp.where(low, other, flat).reshape(count, half, lanes)
    both = jnp.concatenate([even, odd], axis=1)
    return both.reshape(count * 2 * half, lanes).astype(jnp.bfloat16)


def three_terms(values):
    high = values.astype(jnp.bfloat16)
    rest = values - high.astype(jnp.float32)
    middle = rest.astype(jnp.bfloat16)
    low = (rest - middle.astype(jnp.float32)).astype(jnp.bfloat16)
    return [high, middle, low]


def scatter(onehot, values):
    sums = dot(onehot, jnp.concatenate(three_terms(values), axis=1))
    return sums[:, :LANES] + sums[:, LANES : 2 * LANES] + sums[:, 2 * LANES :]


def paired(sums, count, half):
    sums = sums.reshape(count, 2, half, LANES)
    even, odd = sums[:, 0], sums[:, 1]
    return jnp.where(lax.broadcasted_iota(jnp.int32, even.shape, 2) < EDGE, even, odd)


def body(
    rows,
    cols,
    counts_ref,
    pattern_hbm,
    log_rate_hbm,
    state_hbm,
    excess_hbm,
    normal_hbm,
    rate_param_hbm,
    state_param_hbm,
    slip_hbm,
    stiff_hbm,
    damping_hbm,
    blocks_ref,
    final_ref,
    inputs,
    pattern_ref,
    tiles,
    row_pick,
    col_find,
    col_place,
    spread,
    spread_in,
    mirrored,
    weights,
    picked,
    turned,
    row_tab,
    col_tab,
    row_send,
    col_send,
    row_land,
    col_land,
    tile_sem,
    input_sem,
    sems_row_tab,
    sems_col_tab,
    sems_row_part,
    sems_col_part,
):
    my_row = lax.axis_index("row")
    my_col = lax.axis_index("col")
    half = log_rate_hbm.shape[0]
    per_seg = 2 * half
    slots, width = tiles.shape
    groups = tile_sem.shape[0]
    depth = slots // groups

    barrier = pltpu.get_barrier_semaphore()
    for k in range(1, cols):
        pl.semaphore_signal(
            barrier, inc=1, device_id={"col": lax.rem(my_col + k, cols)}, device_id_type=MESH
        )
    for k in range(1, rows):
        pl.semaphore_signal(
            barrier, inc=1, device_id={"row": lax.rem(my_row + k, rows)}, device_id_type=MESH
        )

    def tile_copy(group):
        part = pl.ds(group * depth, depth)
        return pltpu.make_async_copy(blocks_ref.at[part], tiles.at[part], tile_sem.at[group])

    vectors = (
        log_rate_hbm,
        state_hbm,
        excess_hbm,
        normal_hbm,
        rate_param_hbm,
        state_param_hbm,
        slip_hbm,
        stiff_hbm,
        damping_hbm,
    )
    input_copies = [
        pltpu.make_async_copy(vector, inputs.at[index], input_sem.at[index])
        for index, vector in enumerate(vectors)
    ]
    input_copies.append(
        pltpu.make_async_copy(pattern_hbm, pattern_ref, input_sem.at[len(vectors)])
    )
    for copy in input_copies:
        copy.start()
    for group in range(groups):
        tile_copy(group).start()
    for copy in input_copies:
        copy.wait()
    rate_in, state_in, excess_ref, normal_in, rate_param_in = (inputs.at[n] for n in range(5))
    state_param_ref, slip_ref, stiff_ref, damping_in = (inputs.at[n] for n in range(5, 9))
    rate_ref, state_ref, stress_ref, normal_ref, rate_param_ref, damping_ref = (
        final_ref.at[n] for n in range(6)
    )
    rate_ref[...] = rate_in[...]

    row_slot = pattern_ref[0:1, :]
    col_slot = pattern_ref[1:2, :]
    active = lax.broadcasted_iota(jnp.int32, (1, slots), 1) < counts_ref[0, 0]
    diagonal = (col_slot // per_seg == my_row) & (
        row_slot == my_col * per_seg + col_slot % per_seg
    )

    def position(block):
        inner = block % per_seg
        return (block // per_seg) * per_seg + (inner % 2) * half + inner // 2

    def onehot(block, total):
        hit = position(block) == lax.broadcasted_iota(jnp.int32, (total, slots), 0)
        return jnp.where(hit & active, 1.0, 0.0)

    spread[...] = jnp.where(
        lax.broadcasted_iota(jnp.int32, spread.shape, 0)
        == lax.broadcasted_iota(jnp.int32, spread.shape, 1) // EDGE,
        1.0,
        0.0,
    ).astype(jnp.bfloat16)
    def tab_copy(step, axis, k, sender):
        tab, sems, me, count = (
            (row_tab, sems_row_tab, my_col, cols)
            if axis == "col"
            else (col_tab, sems_col_tab, my_row, rows)
        )
        slot = me if sender else lax.rem(me - k + count, count)
        return pltpu.make_async_remote_copy(
            src_ref=tab.at[step, slot],
            dst_ref=tab.at[step, slot],
            send_sem=sems.at[0, step, k],
            recv_sem=sems.at[1, step, k],
            device_id={axis: lax.rem(me + k, count)},
            device_id_type=MESH,
        )

    def part_copy(step, axis, k):
        send, land, sems, me, count = (
            (row_send, row_land, sems_row_part, my_col, cols)
            if axis == "col"
            else (col_send, col_land, sems_col_part, my_row, rows)
        )
        target = lax.rem(me + k, count)
        return pltpu.make_async_remote_copy(
            src_ref=send.at[step, target],
            dst_ref=land.at[step, k - 1],
            send_sem=sems.at[0, step, k],
            recv_sem=sems.at[1, step, k],
            device_id={axis: target},
            device_id_type=MESH,
        )

    pl.semaphore_wait(barrier, rows + cols - 2)

    def one_step(step, carry):
        rate_log = rate_ref[...]
        speed = jnp.exp(rate_log)
        pushed = (speed - 1.0).astype(jnp.bfloat16)
        row_tab[step, my_col] = pushed
        col_tab[step, my_row] = pushed
        for k in range(1, cols):
            tab_copy(step, "col", k, True).start()
        for k in range(1, rows):
            tab_copy(step, "row", k, True).start()

        @pl.when(step == 0)
        def _():
            normal_ref[...] = normal_in[...]
            rate_param_ref[...] = rate_param_in[...]
            damping_ref[...] = damping_in[...]
            rate_log = rate_in[...]
            state = state_in[...]
            rate_param = rate_param_ref[...]
            balance = normal_ref[...] * rate_param * inverse_sinh(
                0.5 * jnp.exp(rate_log + state / rate_param)
            ) + damping_ref[...] * jnp.exp(rate_log)
            state_ref[...] = state
            stress_ref[...] = balance * (1.0 + excess_ref[...])
            row_pick[...] = onehot(row_slot, row_pick.shape[1]).T.astype(jnp.bfloat16)
            found = onehot(col_slot, col_place.shape[0])
            col_find[...] = found.astype(jnp.bfloat16)
            col_place[...] = jnp.where(diagonal, 0.0, found).astype(jnp.bfloat16)
            for group in range(groups):
                tile_copy(group).wait()

        for k in range(1, cols):
            tab_copy(step, "col", k, False).wait_recv()
        row_values = dot(row_pick[...], twice(row_tab[step])).astype(jnp.bfloat16)

        def mirror_turn(turn, carry):
            strip = pl.ds(pl.multiple_of(turn * STRIP, STRIP), STRIP)
            values = spread_in[strip, :]
            total = jnp.zeros((STRIP, LANES), jnp.float32)
            for begin in range(0, width, SPAN):
                part = pl.ds(begin, SPAN)
                product = tiles[strip, part].astype(jnp.float32) * dot(values, spread[:, part])
                for c in range(SPAN // LANES):
                    total = total + product[:, c * LANES : (c + 1) * LANES]
            mirrored[strip, :] = total
            return carry

        spread_in[...] = row_values
        lax.fori_loop(0, slots // STRIP, mirror_turn, 0)
        for k in range(1, rows):
            tab_copy(step, "row", k, False).wait_recv()
        mirror = mirrored[...]
        mirror = mirror + pltpu.roll(mirror, EDGE, 1)
        col_send[step] = paired(scatter(col_place[...], mirror), rows, half)

        values = lax.dot_general(
            twice(col_tab[step]),
            col_find[...],
            (((0,), (0,)), ((), ())),
            preferred_element_type=jnp.float32,
        )[:EDGE]
        section = lax.broadcasted_iota(jnp.int32, (EDGE, LANES), 1) // GROUP
        for base in range(slots // LANES):
            part = values[:, base * LANES : (base + 1) * LANES]
            shifted = [part] + [pltpu.roll(part, n * GROUP, 1) for n in range(1, QUAD)]
            for inner in range(QUAD):
                weights[base * QUAD + inner] = jnp.concatenate(
                    [
                        jnp.where(section == q, shifted[(q - inner) % QUAD], 0.0)
                        for q in range(QUAD)
                    ],
                    axis=0,
                ).astype(jnp.bfloat16)

        for k in range(1, rows):
            part_copy(step, "row", k).start()

        own = lax.broadcasted_iota(jnp.int32, (1, GROUP, LANES), 1) == (
            lax.broadcasted_iota(jnp.int32, (1, GROUP, LANES), 2) % GROUP
        )
        wide = QUAD * EDGE
        fours = width // wide

        def direct_turn(turn, carry):
            for inner in range(BATCH):
                group = turn * BATCH + inner
                part = tiles[pl.ds(pl.multiple_of(group * GROUP, GROUP), GROUP), :]
                stacked = jnp.concatenate(
                    [part[:, n * wide : (n + 1) * wide] for n in range(fours)], axis=0
                )
                product = dot(stacked, weights[group]).reshape(fours, GROUP, LANES)
                picked[group] = jnp.sum(jnp.where(own, product, 0.0), axis=1)
            return carry

        lax.fori_loop(0, slots // (BATCH * GROUP), direct_turn, 0)
        narrow = lax.broadcasted_iota(jnp.int32, (fours, LANES), 1) // GROUP
        pieces = [[] for q in range(QUAD)]
        for base in range(slots // LANES):
            parts = [picked[base * QUAD + inner] for inner in range(QUAD)]
            for q in range(QUAD):
                joined = jnp.zeros((fours, LANES), jnp.float32)
                for inner in range(QUAD):
                    shift = (inner - q) % QUAD * GROUP
                    moved = pltpu.roll(parts[inner], shift, 1) if shift else parts[inner]
                    joined = jnp.where(narrow == inner, moved, joined)
                pieces[q].append(joined)
        direct = jnp.concatenate([jnp.concatenate(part, axis=1) for part in pieces], axis=0)
        sums = dot(jnp.concatenate(three_terms(direct), axis=0), row_pick[...])
        sums = sums[:EDGE] + sums[EDGE : 2 * EDGE] + sums[2 * EDGE :]
        for q in range(QUAD):
            for copied in range(LANES // EDGE):
                for chunk in range(turned.shape[0]):
                    turned[chunk, pl.ds(copied * EDGE + q, fours, QUAD), :] = sums[
                        q * fours : (q + 1) * fours, chunk * LANES : (chunk + 1) * LANES
                    ]
        back = jnp.concatenate([turned[chunk].T for chunk in range(turned.shape[0])], axis=0)
        row_send[step] = paired(back, cols, half)
        for k in range(1, cols):
            part_copy(step, "col", k).start()

        state = state_ref[...]
        state_param = state_param_ref[...]
        new_state = state + time_step * (state_param / slip_ref[...]) * (
            jnp.exp(-state / state_param) - speed
        )
        normal_stress, rate_param, damping = normal_ref[...], rate_param_ref[...], damping_ref[...]
        viscous, friction, slope = resistance(
            rate_log, new_state, normal_stress, rate_param, damping
        )
        for k in range(1, rows):
            tab_copy(step, "row", k, True).wait_send()
        for k in range(1, cols):
            tab_copy(step, "col", k, True).wait_send()
        stress_rate = col_send[step, my_row] + row_send[step, my_col]
        for k in range(1, rows):
            part_copy(step, "row", k).wait_recv()
            stress_rate = stress_rate + col_land[step, k - 1]
        for k in range(1, rows):
            part_copy(step, "row", k).wait_send()
        for k in range(1, cols):
            part_copy(step, "col", k).wait_recv()
            stress_rate = stress_rate + row_land[step, k - 1]
        for k in range(1, cols):
            part_copy(step, "col", k).wait_send()
        stress = stress_ref[...] + time_step * (stress_rate - stiff_ref[...] * (speed - 1.0))
        state_ref[...] = new_state
        stress_ref[...] = stress
        rate_log = rate_log - (stress - viscous - friction) / slope
        rate_ref[...] = rate_log

        @pl.when(step < STEPS - 1)
        def _():
            rate_ref[...] = friction_solve(
                rate_log, stress, new_state, normal_stress, rate_param, damping
            )

        return carry

    lax.fori_loop(0, STEPS, one_step, 0)


def finish(final_ref, rate_ref, state_ref, stress_ref):
    rate_log, state, stress, normal_stress, rate_param, damping = (final_ref[n] for n in range(6))
    state_ref[...] = state
    stress_ref[...] = stress
    rate_ref[...] = friction_solve(rate_log, stress, state, normal_stress, rate_param, damping)


def on_device(*arguments):
    vectors, (blocks, pattern, counts) = arguments[:9], arguments[9:]
    rows = lax.axis_size("row")
    cols = lax.axis_size("col")
    patches = vectors[0].shape[0]
    shape = (patches // LANES, LANES)
    half = shape[0]
    slots, width = blocks.shape[2], blocks.shape[3]
    blocks_row = cols * 2 * half
    blocks_col = rows * 2 * half
    vmem = pl.BlockSpec(memory_space=pltpu.VMEM)
    bf16, f32 = jnp.bfloat16, jnp.float32
    hbm = pl.BlockSpec(memory_space=pltpu.HBM)
    final = pl.pallas_call(
        functools.partial(body, rows, cols),
        out_shape=jax.ShapeDtypeStruct((6,) + shape, f32),
        in_specs=[pl.BlockSpec(memory_space=pltpu.SMEM)] + [hbm] * 11,
        out_specs=vmem,
        scratch_shapes=[
            pltpu.VMEM((9,) + shape, f32),
            pltpu.VMEM((2, slots), jnp.int32),
            pltpu.VMEM((slots, width), bf16),
            pltpu.VMEM((slots, blocks_row), bf16),
            pltpu.VMEM((blocks_col, slots), bf16),
            pltpu.VMEM((blocks_col, slots), bf16),
            pltpu.VMEM((LANES, width), bf16),
            pltpu.VMEM((slots, LANES), bf16),
            pltpu.VMEM((slots, LANES), f32),
            pltpu.VMEM((slots // GROUP, QUAD * EDGE, LANES), bf16),
            pltpu.VMEM((slots // GROUP, width // (QUAD * EDGE), LANES), f32),
            pltpu.VMEM((blocks_row // LANES, LANES, LANES), f32),
            pltpu.VMEM((STEPS, cols) + shape, bf16),
            pltpu.VMEM((STEPS, rows) + shape, bf16),
            pltpu.VMEM((STEPS, cols) + shape, f32),
            pltpu.VMEM((STEPS, rows) + shape, f32),
            pltpu.VMEM((STEPS, cols - 1) + shape, f32),
            pltpu.VMEM((STEPS, rows - 1) + shape, f32),
            pltpu.SemaphoreType.DMA((4,)),
            pltpu.SemaphoreType.DMA((10,)),
            pltpu.SemaphoreType.DMA((2, STEPS, cols)),
            pltpu.SemaphoreType.DMA((2, STEPS, rows)),
            pltpu.SemaphoreType.DMA((2, STEPS, cols)),
            pltpu.SemaphoreType.DMA((2, STEPS, rows)),
        ],
        compiler_params=pltpu.CompilerParams(
            collective_id=0, has_side_effects=True, vmem_limit_bytes=60 * 1024 * 1024
        ),
    )(
        counts,
        pattern.reshape(slots, 2).T,
        *[vector.reshape(shape) for vector in vectors],
        blocks.reshape(slots, width),
    )
    outputs = pl.pallas_call(
        finish,
        out_shape=[jax.ShapeDtypeStruct(shape, f32)] * 3,
        in_specs=[vmem],
        out_specs=[vmem] * 3,
    )(final)
    return tuple(output.reshape(patches) for output in outputs)


def solution(mesh):
    patches = P(("row", "col"))
    in_specs = (patches,) * 9 + (
        P("row", "col", None, None),
        P("row", "col", None, None),
        P("row", "col"),
    )
    return jax.shard_map(
        on_device, mesh=mesh, in_specs=in_specs, out_specs=(patches,) * 3, check_vma=False
    )
```

```python
import functools

import jax
import jax.numpy as jnp
from jax import lax
from jax.experimental import pallas as pl
from jax.experimental.pallas import tpu as pltpu
from jax.sharding import PartitionSpec as P

STEPS = 2
NEWTON = 4
EDGE = 64
LANES = 128
SPAN = 256
STRIP = 256
QUAD = 4
GROUP = LANES // QUAD
MESH = pl.DeviceIdType.MESH

time_step = 0.25


def inverse_sinh(value):
    return jnp.log(value + jnp.sqrt(1.0 + value * value))


def resistance(rate_log, state, normal_stress, rate_param, damping):
    speed = jnp.exp(rate_log)
    ratio = 0.5 * jnp.exp(rate_log + state / rate_param)
    slope = -damping * speed - normal_stress * rate_param * ratio / jnp.sqrt(1.0 + ratio * ratio)
    return damping * speed, normal_stress * rate_param * inverse_sinh(ratio), slope


def friction_solve(rate_log, stress, state, normal_stress, rate_param, damping):
    for turn_index in range(NEWTON - 1):
        viscous, friction, slope = resistance(rate_log, state, normal_stress, rate_param, damping)
        rate_log = rate_log - (stress - viscous - friction) / slope
    return rate_log


def dot(left, right):
    return jnp.dot(left, right, preferred_element_type=jnp.float32)


def twice(pieces):
    count, half, lanes = pieces.shape
    flat = pieces.astype(jnp.float32).reshape(count * half, lanes)
    other = pltpu.roll(flat, EDGE, 1)
    low = lax.broadcasted_iota(jnp.int32, flat.shape, 1) < EDGE
    even = jnp.where(low, flat, other).reshape(count, half, lanes)
    odd = jnp.where(low, other, flat).reshape(count, half, lanes)
    both = jnp.concatenate([even, odd], axis=1)
    return both.reshape(count * 2 * half, lanes).astype(jnp.bfloat16)


def three_terms(values):
    high = values.astype(jnp.bfloat16)
    rest = values - high.astype(jnp.float32)
    middle = rest.astype(jnp.bfloat16)
    low = (rest - middle.astype(jnp.float32)).astype(jnp.bfloat16)
    return [high, middle, low]


def scatter(onehot, values):
    sums = dot(onehot, jnp.concatenate(three_terms(values), axis=1))
    return sums[:, :LANES] + sums[:, LANES : 2 * LANES] + sums[:, 2 * LANES :]


def paired(sums, count, half):
    sums = sums.reshape(count, 2, half, LANES)
    even, odd = sums[:, 0], sums[:, 1]
    return jnp.where(lax.broadcasted_iota(jnp.int32, even.shape, 2) < EDGE, even, odd)


def body(
    rows,
    cols,
    counts_ref,
    pattern_hbm,
    log_rate_hbm,
    state_hbm,
    excess_hbm,
    normal_hbm,
    rate_param_hbm,
    state_param_hbm,
    slip_hbm,
    stiff_hbm,
    damping_hbm,
    blocks_ref,
    final_ref,
    inputs,
    pattern_ref,
    tiles,
    row_pick,
    col_find,
    col_place,
    spread,
    turned,
    row_tab,
    col_tab,
    row_send,
    col_send,
    row_land,
    col_land,
    tile_sem,
    input_sem,
    sems_row_tab,
    sems_col_tab,
    sems_row_part,
    sems_col_part,
):
    my_row = lax.axis_index("row")
    my_col = lax.axis_index("col")
    half = log_rate_hbm.shape[0]
    per_seg = 2 * half
    slots, width = tiles.shape
    groups = tile_sem.shape[0]
    depth = slots // groups

    barrier = pltpu.get_barrier_semaphore()
    for k in range(1, cols):
        pl.semaphore_signal(
            barrier, inc=1, device_id={"col": lax.rem(my_col + k, cols)}, device_id_type=MESH
        )
    for k in range(1, rows):
        pl.semaphore_signal(
            barrier, inc=1, device_id={"row": lax.rem(my_row + k, rows)}, device_id_type=MESH
        )

    def tile_copy(group):
        part = pl.ds(group * depth, depth)
        return pltpu.make_async_copy(blocks_ref.at[part], tiles.at[part], tile_sem.at[group])

    vectors = (
        log_rate_hbm,
        state_hbm,
        excess_hbm,
        normal_hbm,
        rate_param_hbm,
        state_param_hbm,
        slip_hbm,
        stiff_hbm,
        damping_hbm,
    )
    input_copies = [
        pltpu.make_async_copy(vector, inputs.at[index], input_sem.at[index])
        for index, vector in enumerate(vectors)
    ]
    input_copies.append(
        pltpu.make_async_copy(pattern_hbm, pattern_ref, input_sem.at[len(vectors)])
    )
    for copy in input_copies:
        copy.start()
    for group in range(groups):
        tile_copy(group).start()
    for copy in input_copies:
        copy.wait()
    rate_in, state_in, excess_ref, normal_in, rate_param_in = (inputs.at[n] for n in range(5))
    state_param_ref, slip_ref, stiff_ref, damping_in = (inputs.at[n] for n in range(5, 9))
    rate_ref, state_ref, stress_ref, normal_ref, rate_param_ref, damping_ref = (
        final_ref.at[n] for n in range(6)
    )
    rate_ref[...] = rate_in[...]

    row_slot = pattern_ref[0:1, :]
    col_slot = pattern_ref[1:2, :]
    active = lax.broadcasted_iota(jnp.int32, (1, slots), 1) < counts_ref[0, 0]
    diagonal = (col_slot // per_seg == my_row) & (
        row_slot == my_col * per_seg + col_slot % per_seg
    )

    def position(block):
        inner = block % per_seg
        return (block // per_seg) * per_seg + (inner % 2) * half + inner // 2

    def onehot(block, total):
        hit = position(block) == lax.broadcasted_iota(jnp.int32, (total, slots), 0)
        return jnp.where(hit & active, 1.0, 0.0)

    spread[...] = jnp.where(
        lax.broadcasted_iota(jnp.int32, spread.shape, 0)
        == lax.broadcasted_iota(jnp.int32, spread.shape, 1) // EDGE,
        1.0,
        0.0,
    ).astype(jnp.bfloat16)
    def tab_copy(step, axis, k, sender):
        tab, sems, me, count = (
            (row_tab, sems_row_tab, my_col, cols)
            if axis == "col"
            else (col_tab, sems_col_tab, my_row, rows)
        )
        slot = me if sender else lax.rem(me - k + count, count)
        return pltpu.make_async_remote_copy(
            src_ref=tab.at[step, slot],
            dst_ref=tab.at[step, slot],
            send_sem=sems.at[0, step, k],
            recv_sem=sems.at[1, step, k],
            device_id={axis: lax.rem(me + k, count)},
            device_id_type=MESH,
        )

    def part_copy(step, axis, k):
        send, land, sems, me, count = (
            (row_send, row_land, sems_row_part, my_col, cols)
            if axis == "col"
            else (col_send, col_land, sems_col_part, my_row, rows)
        )
        target = lax.rem(me + k, count)
        return pltpu.make_async_remote_copy(
            src_ref=send.at[step, target],
            dst_ref=land.at[step, k - 1],
            send_sem=sems.at[0, step, k],
            recv_sem=sems.at[1, step, k],
            device_id={axis: target},
            device_id_type=MESH,
        )

    pl.semaphore_wait(barrier, rows + cols - 2)

    def one_step(step, carry):
        rate_log = rate_ref[...]
        speed = jnp.exp(rate_log)
        pushed = (speed - 1.0).astype(jnp.bfloat16)
        row_tab[step, my_col] = pushed
        col_tab[step, my_row] = pushed
        for k in range(1, cols):
            tab_copy(step, "col", k, True).start()
        for k in range(1, rows):
            tab_copy(step, "row", k, True).start()

        @pl.when(step == 0)
        def _():
            normal_ref[...] = normal_in[...]
            rate_param_ref[...] = rate_param_in[...]
            damping_ref[...] = damping_in[...]
            rate_log = rate_in[...]
            state = state_in[...]
            rate_param = rate_param_ref[...]
            balance = normal_ref[...] * rate_param * inverse_sinh(
                0.5 * jnp.exp(rate_log + state / rate_param)
            ) + damping_ref[...] * jnp.exp(rate_log)
            state_ref[...] = state
            stress_ref[...] = balance * (1.0 + excess_ref[...])
            row_pick[...] = onehot(row_slot, row_pick.shape[1]).T.astype(jnp.bfloat16)
            found = onehot(col_slot, col_place.shape[0])
            col_find[...] = found.astype(jnp.bfloat16)
            col_place[...] = jnp.where(diagonal, 0.0, found).astype(jnp.bfloat16)
            for group in range(groups):
                tile_copy(group).wait()

        for k in range(1, cols):
            tab_copy(step, "col", k, False).wait_recv()
        row_values = dot(row_pick[...], twice(row_tab[step])).astype(jnp.bfloat16)

        mirror = []
        for first in range(0, slots, STRIP):
            strip = pl.ds(first, STRIP)
            values = row_values[first : first + STRIP]
            total = jnp.zeros((STRIP, LANES), jnp.float32)
            for begin in range(0, width, SPAN):
                part = pl.ds(begin, SPAN)
                product = tiles[strip, part].astype(jnp.float32) * dot(values, spread[:, part])
                for c in range(SPAN // LANES):
                    total = total + product[:, c * LANES : (c + 1) * LANES]
            mirror.append(total)
        mirror = jnp.concatenate(mirror, axis=0)
        for k in range(1, rows):
            tab_copy(step, "row", k, False).wait_recv()
        mirror = mirror + pltpu.roll(mirror, EDGE, 1)
        col_send[step] = paired(scatter(col_place[...], mirror), rows, half)

        for k in range(1, rows):
            part_copy(step, "row", k).start()
        values = lax.dot_general(
            twice(col_tab[step]),
            col_find[...],
            (((0,), (0,)), ((), ())),
            preferred_element_type=jnp.float32,
        )[:EDGE]
        section = lax.broadcasted_iota(jnp.int32, (EDGE, LANES), 1) // GROUP
        own = lax.broadcasted_iota(jnp.int32, (1, GROUP, LANES), 1) == (
            lax.broadcasted_iota(jnp.int32, (1, GROUP, LANES), 2) % GROUP
        )
        wide = QUAD * EDGE
        fours = width // wide
        narrow = lax.broadcasted_iota(jnp.int32, (fours, LANES), 1) // GROUP
        sums = jnp.zeros((3 * EDGE, row_pick.shape[1]), jnp.float32)
        for base in range(0, slots, LANES):
            part = values[:, base : base + LANES]
            shifted = [part] + [pltpu.roll(part, n * GROUP, 1) for n in range(1, QUAD)]
            picked = []
            for inner in range(QUAD):
                weights = jnp.concatenate(
                    [
                        jnp.where(section == q, shifted[(q - inner) % QUAD], 0.0)
                        for q in range(QUAD)
                    ],
                    axis=0,
                ).astype(jnp.bfloat16)
                group = tiles[pl.ds(base + inner * GROUP, GROUP), :]
                stacked = jnp.concatenate(
                    [group[:, n * wide : (n + 1) * wide] for n in range(fours)], axis=0
                )
                product = dot(stacked, weights).reshape(fours, GROUP, LANES)
                picked.append(jnp.sum(jnp.where(own, product, 0.0), axis=1))
            pieces = []
            for q in range(QUAD):
                joined = jnp.zeros((fours, LANES), jnp.float32)
                for inner in range(QUAD):
                    shift = (inner - q) % QUAD * GROUP
                    moved = pltpu.roll(picked[inner], shift, 1) if shift else picked[inner]
                    joined = jnp.where(narrow == inner, moved, joined)
                pieces.append(joined)
            direct = jnp.concatenate(pieces, axis=0)
            sums = sums + dot(
                jnp.concatenate(three_terms(direct), axis=0), row_pick[pl.ds(base, LANES), :]
            )
        sums = sums[:EDGE] + sums[EDGE : 2 * EDGE] + sums[2 * EDGE :]
        for q in range(QUAD):
            for copied in range(LANES // EDGE):
                for chunk in range(turned.shape[0]):
                    turned[chunk, pl.ds(copied * EDGE + q, fours, QUAD), :] = sums[
                        q * fours : (q + 1) * fours, chunk * LANES : (chunk + 1) * LANES
                    ]
        back = jnp.concatenate([turned[chunk].T for chunk in range(turned.shape[0])], axis=0)
        row_send[step] = paired(back, cols, half)
        for k in range(1, cols):
            part_copy(step, "col", k).start()

        state = state_ref[...]
        state_param = state_param_ref[...]
        new_state = state + time_step * (state_param / slip_ref[...]) * (
            jnp.exp(-state / state_param) - speed
        )
        normal_stress, rate_param, damping = normal_ref[...], rate_param_ref[...], damping_ref[...]
        viscous, friction, slope = resistance(
            rate_log, new_state, normal_stress, rate_param, damping
        )
        for k in range(1, rows):
            tab_copy(step, "row", k, True).wait_send()
        for k in range(1, cols):
            tab_copy(step, "col", k, True).wait_send()
        stress_rate = col_send[step, my_row] + row_send[step, my_col]
        for k in range(1, rows):
            part_copy(step, "row", k).wait_recv()
            stress_rate = stress_rate + col_land[step, k - 1]
        for k in range(1, rows):
            part_copy(step, "row", k).wait_send()
        for k in range(1, cols):
            part_copy(step, "col", k).wait_recv()
            stress_rate = stress_rate + row_land[step, k - 1]
        for k in range(1, cols):
            part_copy(step, "col", k).wait_send()
        stress = stress_ref[...] + time_step * (stress_rate - stiff_ref[...] * (speed - 1.0))
        state_ref[...] = new_state
        stress_ref[...] = stress
        rate_log = rate_log - (stress - viscous - friction) / slope
        rate_ref[...] = rate_log

        @pl.when(step < STEPS - 1)
        def _():
            rate_ref[...] = friction_solve(
                rate_log, stress, new_state, normal_stress, rate_param, damping
            )

        return carry

    lax.fori_loop(0, STEPS, one_step, 0)


def finish(final_ref, rate_ref, state_ref, stress_ref):
    rate_log, state, stress, normal_stress, rate_param, damping = (final_ref[n] for n in range(6))
    state_ref[...] = state
    stress_ref[...] = stress
    rate_ref[...] = friction_solve(rate_log, stress, state, normal_stress, rate_param, damping)


def on_device(*arguments):
    vectors, (blocks, pattern, counts) = arguments[:9], arguments[9:]
    rows = lax.axis_size("row")
    cols = lax.axis_size("col")
    patches = vectors[0].shape[0]
    shape = (patches // LANES, LANES)
    half = shape[0]
    slots, width = blocks.shape[2], blocks.shape[3]
    blocks_row = cols * 2 * half
    blocks_col = rows * 2 * half
    vmem = pl.BlockSpec(memory_space=pltpu.VMEM)
    bf16, f32 = jnp.bfloat16, jnp.float32
    hbm = pl.BlockSpec(memory_space=pltpu.HBM)
    final = pl.pallas_call(
        functools.partial(body, rows, cols),
        out_shape=jax.ShapeDtypeStruct((6,) + shape, f32),
        in_specs=[pl.BlockSpec(memory_space=pltpu.SMEM)] + [hbm] * 11,
        out_specs=vmem,
        scratch_shapes=[
            pltpu.VMEM((9,) + shape, f32),
            pltpu.VMEM((2, slots), jnp.int32),
            pltpu.VMEM((slots, width), bf16),
            pltpu.VMEM((slots, blocks_row), bf16),
            pltpu.VMEM((blocks_col, slots), bf16),
            pltpu.VMEM((blocks_col, slots), bf16),
            pltpu.VMEM((LANES, width), bf16),
            pltpu.VMEM((blocks_row // LANES, LANES, LANES), f32),
            pltpu.VMEM((STEPS, cols) + shape, bf16),
            pltpu.VMEM((STEPS, rows) + shape, bf16),
            pltpu.VMEM((STEPS, cols) + shape, f32),
            pltpu.VMEM((STEPS, rows) + shape, f32),
            pltpu.VMEM((STEPS, cols - 1) + shape, f32),
            pltpu.VMEM((STEPS, rows - 1) + shape, f32),
            pltpu.SemaphoreType.DMA((4,)),
            pltpu.SemaphoreType.DMA((10,)),
            pltpu.SemaphoreType.DMA((2, STEPS, cols)),
            pltpu.SemaphoreType.DMA((2, STEPS, rows)),
            pltpu.SemaphoreType.DMA((2, STEPS, cols)),
            pltpu.SemaphoreType.DMA((2, STEPS, rows)),
        ],
        compiler_params=pltpu.CompilerParams(
            collective_id=0, has_side_effects=True, vmem_limit_bytes=60 * 1024 * 1024
        ),
    )(
        counts,
        pattern.reshape(slots, 2).T,
        *[vector.reshape(shape) for vector in vectors],
        blocks.reshape(slots, width),
    )
    outputs = pl.pallas_call(
        finish,
        out_shape=[jax.ShapeDtypeStruct(shape, f32)] * 3,
        in_specs=[vmem],
        out_specs=[vmem] * 3,
    )(final)
    return tuple(output.reshape(patches) for output in outputs)


def solution(mesh):
    patches = P(("row", "col"))
    in_specs = (patches,) * 9 + (
        P("row", "col", None, None),
        P("row", "col", None, None),
        P("row", "col"),
    )
    return jax.shard_map(
        on_device, mesh=mesh, in_specs=in_specs, out_specs=(patches,) * 3, check_vma=False
    )
```

```python
import functools

import jax
import jax.numpy as jnp
from jax import lax
from jax.experimental import pallas as pl
from jax.experimental.pallas import tpu as pltpu
from jax.sharding import PartitionSpec as P

STEPS = 2
NEWTON = 4
EDGE = 64
LANES = 128
SPAN = 256
STRIP = 256
QUAD = 4
GROUP = LANES // QUAD
MESH = pl.DeviceIdType.MESH

time_step = 0.25


def inverse_sinh(value):
    return jnp.log(value + jnp.sqrt(1.0 + value * value))


def resistance(rate_log, state, normal_stress, rate_param, damping):
    speed = jnp.exp(rate_log)
    ratio = 0.5 * jnp.exp(rate_log + state / rate_param)
    slope = -damping * speed - normal_stress * rate_param * ratio / jnp.sqrt(1.0 + ratio * ratio)
    return damping * speed, normal_stress * rate_param * inverse_sinh(ratio), slope


def friction_solve(rate_log, stress, state, normal_stress, rate_param, damping):
    for turn_index in range(NEWTON - 1):
        viscous, friction, slope = resistance(rate_log, state, normal_stress, rate_param, damping)
        rate_log = rate_log - (stress - viscous - friction) / slope
    return rate_log


def dot(left, right):
    return jnp.dot(left, right, preferred_element_type=jnp.float32)


def twice(pieces):
    count, half, lanes = pieces.shape
    flat = pieces.astype(jnp.float32).reshape(count * half, lanes)
    other = pltpu.roll(flat, EDGE, 1)
    low = lax.broadcasted_iota(jnp.int32, flat.shape, 1) < EDGE
    even = jnp.where(low, flat, other).reshape(count, half, lanes)
    odd = jnp.where(low, other, flat).reshape(count, half, lanes)
    both = jnp.concatenate([even, odd], axis=1)
    return both.reshape(count * 2 * half, lanes).astype(jnp.bfloat16)


def three_terms(values):
    high = values.astype(jnp.bfloat16)
    rest = values - high.astype(jnp.float32)
    middle = rest.astype(jnp.bfloat16)
    low = (rest - middle.astype(jnp.float32)).astype(jnp.bfloat16)
    return [high, middle, low]


def scatter(onehot, values):
    sums = dot(onehot, jnp.concatenate(three_terms(values), axis=1))
    return sums[:, :LANES] + sums[:, LANES : 2 * LANES] + sums[:, 2 * LANES :]


def paired(sums, count, half):
    sums = sums.reshape(count, 2, half, LANES)
    even, odd = sums[:, 0], sums[:, 1]
    return jnp.where(lax.broadcasted_iota(jnp.int32, even.shape, 2) < EDGE, even, odd)


def body(
    rows,
    cols,
    counts_ref,
    pattern_hbm,
    log_rate_hbm,
    state_hbm,
    excess_hbm,
    normal_hbm,
    rate_param_hbm,
    state_param_hbm,
    slip_hbm,
    stiff_hbm,
    damping_hbm,
    blocks_ref,
    final_ref,
    inputs,
    pattern_ref,
    tiles,
    row_pick,
    col_find,
    col_place,
    spread,
    turned,
    row_tab,
    col_tab,
    row_send,
    col_send,
    row_land,
    col_land,
    tile_sem,
    input_sem,
    sems_row_tab,
    sems_col_tab,
    sems_row_part,
    sems_col_part,
):
    my_row = lax.axis_index("row")
    my_col = lax.axis_index("col")
    half = log_rate_hbm.shape[0]
    per_seg = 2 * half
    slots, width = tiles.shape
    groups = tile_sem.shape[0]
    depth = slots // groups

    barrier = pltpu.get_barrier_semaphore()
    for k in range(1, cols):
        pl.semaphore_signal(
            barrier, inc=1, device_id={"col": lax.rem(my_col + k, cols)}, device_id_type=MESH
        )
    for k in range(1, rows):
        pl.semaphore_signal(
            barrier, inc=1, device_id={"row": lax.rem(my_row + k, rows)}, device_id_type=MESH
        )

    def tile_copy(group):
        part = pl.ds(group * depth, depth)
        return pltpu.make_async_copy(blocks_ref.at[part], tiles.at[part], tile_sem.at[group])

    vectors = (
        log_rate_hbm,
        state_hbm,
        excess_hbm,
        normal_hbm,
        rate_param_hbm,
        state_param_hbm,
        slip_hbm,
        stiff_hbm,
        damping_hbm,
    )
    input_copies = [
        pltpu.make_async_copy(vector, inputs.at[index], input_sem.at[index])
        for index, vector in enumerate(vectors)
    ]
    input_copies.append(
        pltpu.make_async_copy(pattern_hbm, pattern_ref, input_sem.at[len(vectors)])
    )
    for copy in input_copies:
        copy.start()
    for group in range(groups):
        tile_copy(group).start()
    input_copies[0].wait()
    rate_in, state_in, excess_ref, normal_in, rate_param_in = (inputs.at[n] for n in range(5))
    state_param_ref, slip_ref, stiff_ref, damping_in = (inputs.at[n] for n in range(5, 9))
    rate_ref, state_ref, stress_ref, normal_ref, rate_param_ref, damping_ref = (
        final_ref.at[n] for n in range(6)
    )
    rate_ref[...] = rate_in[...]

    def tab_copy(step, axis, k, sender):
        tab, sems, me, count = (
            (row_tab, sems_row_tab, my_col, cols)
            if axis == "col"
            else (col_tab, sems_col_tab, my_row, rows)
        )
        slot = me if sender else lax.rem(me - k + count, count)
        return pltpu.make_async_remote_copy(
            src_ref=tab.at[step, slot],
            dst_ref=tab.at[step, slot],
            send_sem=sems.at[0, step, k],
            recv_sem=sems.at[1, step, k],
            device_id={axis: lax.rem(me + k, count)},
            device_id_type=MESH,
        )

    def part_copy(step, axis, k):
        send, land, sems, me, count = (
            (row_send, row_land, sems_row_part, my_col, cols)
            if axis == "col"
            else (col_send, col_land, sems_col_part, my_row, rows)
        )
        target = lax.rem(me + k, count)
        return pltpu.make_async_remote_copy(
            src_ref=send.at[step, target],
            dst_ref=land.at[step, k - 1],
            send_sem=sems.at[0, step, k],
            recv_sem=sems.at[1, step, k],
            device_id={axis: target},
            device_id_type=MESH,
        )

    pl.semaphore_wait(barrier, rows + cols - 2)

    def one_step(step, carry):
        rate_log = rate_ref[...]
        speed = jnp.exp(rate_log)
        pushed = (speed - 1.0).astype(jnp.bfloat16)
        row_tab[step, my_col] = pushed
        col_tab[step, my_row] = pushed
        for k in range(1, cols):
            tab_copy(step, "col", k, True).start()
        for k in range(1, rows):
            tab_copy(step, "row", k, True).start()

        @pl.when(step == 0)
        def _():
            for copy in input_copies[1:]:
                copy.wait()
            row_slot = pattern_ref[0:1, :]
            col_slot = pattern_ref[1:2, :]
            active = lax.broadcasted_iota(jnp.int32, (1, slots), 1) < counts_ref[0, 0]
            diagonal = (col_slot // per_seg == my_row) & (
                row_slot == my_col * per_seg + col_slot % per_seg
            )

            def position(block):
                inner = block % per_seg
                return (block // per_seg) * per_seg + (inner % 2) * half + inner // 2

            def onehot(block, total):
                hit = position(block) == lax.broadcasted_iota(jnp.int32, (total, slots), 0)
                return jnp.where(hit & active, 1.0, 0.0)

            spread[...] = jnp.where(
                lax.broadcasted_iota(jnp.int32, spread.shape, 0)
                == lax.broadcasted_iota(jnp.int32, spread.shape, 1) // EDGE,
                1.0,
                0.0,
            ).astype(jnp.bfloat16)
            normal_ref[...] = normal_in[...]
            rate_param_ref[...] = rate_param_in[...]
            damping_ref[...] = damping_in[...]
            rate_log = rate_in[...]
            state = state_in[...]
            rate_param = rate_param_ref[...]
            balance = normal_ref[...] * rate_param * inverse_sinh(
                0.5 * jnp.exp(rate_log + state / rate_param)
            ) + damping_ref[...] * jnp.exp(rate_log)
            state_ref[...] = state
            stress_ref[...] = balance * (1.0 + excess_ref[...])
            row_pick[...] = onehot(row_slot, row_pick.shape[1]).T.astype(jnp.bfloat16)
            found = onehot(col_slot, col_place.shape[0])
            col_find[...] = found.astype(jnp.bfloat16)
            col_place[...] = jnp.where(diagonal, 0.0, found).astype(jnp.bfloat16)
            for group in range(groups):
                tile_copy(group).wait()

        for k in range(1, cols):
            tab_copy(step, "col", k, False).wait_recv()
        row_values = dot(row_pick[...], twice(row_tab[step])).astype(jnp.bfloat16)

        mirror = []
        for first in range(0, slots, STRIP):
            strip = pl.ds(first, STRIP)
            values = row_values[first : first + STRIP]
            total = jnp.zeros((STRIP, LANES), jnp.float32)
            for begin in range(0, width, SPAN):
                part = pl.ds(begin, SPAN)
                product = tiles[strip, part].astype(jnp.float32) * dot(values, spread[:, part])
                for c in range(SPAN // LANES):
                    total = total + product[:, c * LANES : (c + 1) * LANES]
            mirror.append(total)
        mirror = jnp.concatenate(mirror, axis=0)
        for k in range(1, rows):
            tab_copy(step, "row", k, False).wait_recv()
        mirror = mirror + pltpu.roll(mirror, EDGE, 1)
        col_send[step] = paired(scatter(col_place[...], mirror), rows, half)

        for k in range(1, rows):
            part_copy(step, "row", k).start()
        values = lax.dot_general(
            twice(col_tab[step]),
            col_find[...],
            (((0,), (0,)), ((), ())),
            preferred_element_type=jnp.float32,
        )[:EDGE]
        section = lax.broadcasted_iota(jnp.int32, (EDGE, LANES), 1) // GROUP
        own = lax.broadcasted_iota(jnp.int32, (1, GROUP, LANES), 1) == (
            lax.broadcasted_iota(jnp.int32, (1, GROUP, LANES), 2) % GROUP
        )
        wide = QUAD * EDGE
        fours = width // wide
        narrow = lax.broadcasted_iota(jnp.int32, (fours, LANES), 1) // GROUP
        sums = jnp.zeros((3 * EDGE, row_pick.shape[1]), jnp.float32)
        for base in range(0, slots, LANES):
            part = values[:, base : base + LANES]
            shifted = [part] + [pltpu.roll(part, n * GROUP, 1) for n in range(1, QUAD)]
            picked = []
            for inner in range(QUAD):
                weights = jnp.concatenate(
                    [
                        jnp.where(section == q, shifted[(q - inner) % QUAD], 0.0)
                        for q in range(QUAD)
                    ],
                    axis=0,
                ).astype(jnp.bfloat16)
                group = tiles[pl.ds(base + inner * GROUP, GROUP), :]
                stacked = jnp.concatenate(
                    [group[:, n * wide : (n + 1) * wide] for n in range(fours)], axis=0
                )
                product = dot(stacked, weights).reshape(fours, GROUP, LANES)
                picked.append(jnp.sum(jnp.where(own, product, 0.0), axis=1))
            pieces = []
            for q in range(QUAD):
                joined = jnp.zeros((fours, LANES), jnp.float32)
                for inner in range(QUAD):
                    shift = (inner - q) % QUAD * GROUP
                    moved = pltpu.roll(picked[inner], shift, 1) if shift else picked[inner]
                    joined = jnp.where(narrow == inner, moved, joined)
                pieces.append(joined)
            direct = jnp.concatenate(pieces, axis=0)
            sums = sums + dot(
                jnp.concatenate(three_terms(direct), axis=0), row_pick[pl.ds(base, LANES), :]
            )
        sums = sums[:EDGE] + sums[EDGE : 2 * EDGE] + sums[2 * EDGE :]
        for q in range(QUAD):
            for copied in range(LANES // EDGE):
                for chunk in range(turned.shape[0]):
                    turned[chunk, pl.ds(copied * EDGE + q, fours, QUAD), :] = sums[
                        q * fours : (q + 1) * fours, chunk * LANES : (chunk + 1) * LANES
                    ]
        back = jnp.concatenate([turned[chunk].T for chunk in range(turned.shape[0])], axis=0)
        row_send[step] = paired(back, cols, half)
        for k in range(1, cols):
            part_copy(step, "col", k).start()

        state = state_ref[...]
        state_param = state_param_ref[...]
        new_state = state + time_step * (state_param / slip_ref[...]) * (
            jnp.exp(-state / state_param) - speed
        )
        normal_stress, rate_param, damping = normal_ref[...], rate_param_ref[...], damping_ref[...]
        viscous, friction, slope = resistance(
            rate_log, new_state, normal_stress, rate_param, damping
        )
        for k in range(1, rows):
            tab_copy(step, "row", k, True).wait_send()
        for k in range(1, cols):
            tab_copy(step, "col", k, True).wait_send()
        stress_rate = col_send[step, my_row] + row_send[step, my_col]
        for k in range(1, rows):
            part_copy(step, "row", k).wait_recv()
            stress_rate = stress_rate + col_land[step, k - 1]
        for k in range(1, rows):
            part_copy(step, "row", k).wait_send()
        for k in range(1, cols):
            part_copy(step, "col", k).wait_recv()
            stress_rate = stress_rate + row_land[step, k - 1]
        for k in range(1, cols):
            part_copy(step, "col", k).wait_send()
        stress = stress_ref[...] + time_step * (stress_rate - stiff_ref[...] * (speed - 1.0))
        state_ref[...] = new_state
        stress_ref[...] = stress
        rate_log = rate_log - (stress - viscous - friction) / slope
        rate_ref[...] = rate_log

        @pl.when(step < STEPS - 1)
        def _():
            rate_ref[...] = friction_solve(
                rate_log, stress, new_state, normal_stress, rate_param, damping
            )

        return carry

    lax.fori_loop(0, STEPS, one_step, 0)


def finish(final_ref, rate_ref, state_ref, stress_ref):
    rate_log, state, stress, normal_stress, rate_param, damping = (final_ref[n] for n in range(6))
    state_ref[...] = state
    stress_ref[...] = stress
    rate_ref[...] = friction_solve(rate_log, stress, state, normal_stress, rate_param, damping)


def on_device(*arguments):
    vectors, (blocks, pattern, counts) = arguments[:9], arguments[9:]
    rows = lax.axis_size("row")
    cols = lax.axis_size("col")
    patches = vectors[0].shape[0]
    shape = (patches // LANES, LANES)
    half = shape[0]
    slots, width = blocks.shape[2], blocks.shape[3]
    blocks_row = cols * 2 * half
    blocks_col = rows * 2 * half
    vmem = pl.BlockSpec(memory_space=pltpu.VMEM)
    bf16, f32 = jnp.bfloat16, jnp.float32
    hbm = pl.BlockSpec(memory_space=pltpu.HBM)
    final = pl.pallas_call(
        functools.partial(body, rows, cols),
        out_shape=jax.ShapeDtypeStruct((6,) + shape, f32),
        in_specs=[pl.BlockSpec(memory_space=pltpu.SMEM)] + [hbm] * 11,
        out_specs=vmem,
        scratch_shapes=[
            pltpu.VMEM((9,) + shape, f32),
            pltpu.VMEM((2, slots), jnp.int32),
            pltpu.VMEM((slots, width), bf16),
            pltpu.VMEM((slots, blocks_row), bf16),
            pltpu.VMEM((blocks_col, slots), bf16),
            pltpu.VMEM((blocks_col, slots), bf16),
            pltpu.VMEM((LANES, width), bf16),
            pltpu.VMEM((blocks_row // LANES, LANES, LANES), f32),
            pltpu.VMEM((STEPS, cols) + shape, bf16),
            pltpu.VMEM((STEPS, rows) + shape, bf16),
            pltpu.VMEM((STEPS, cols) + shape, f32),
            pltpu.VMEM((STEPS, rows) + shape, f32),
            pltpu.VMEM((STEPS, cols - 1) + shape, f32),
            pltpu.VMEM((STEPS, rows - 1) + shape, f32),
            pltpu.SemaphoreType.DMA((4,)),
            pltpu.SemaphoreType.DMA((10,)),
            pltpu.SemaphoreType.DMA((2, STEPS, cols)),
            pltpu.SemaphoreType.DMA((2, STEPS, rows)),
            pltpu.SemaphoreType.DMA((2, STEPS, cols)),
            pltpu.SemaphoreType.DMA((2, STEPS, rows)),
        ],
        compiler_params=pltpu.CompilerParams(
            collective_id=0, has_side_effects=True, vmem_limit_bytes=60 * 1024 * 1024
        ),
    )(
        counts,
        pattern.reshape(slots, 2).T,
        *[vector.reshape(shape) for vector in vectors],
        blocks.reshape(slots, width),
    )
    outputs = pl.pallas_call(
        finish,
        out_shape=[jax.ShapeDtypeStruct(shape, f32)] * 3,
        in_specs=[vmem],
        out_specs=[vmem] * 3,
    )(final)
    return tuple(output.reshape(patches) for output in outputs)


def solution(mesh):
    patches = P(("row", "col"))
    in_specs = (patches,) * 9 + (
        P("row", "col", None, None),
        P("row", "col", None, None),
        P("row", "col"),
    )
    return jax.shard_map(
        on_device, mesh=mesh, in_specs=in_specs, out_specs=(patches,) * 3, check_vma=False
    )
```
